512 devices in a mesh: dev: 128 (over z, y, core), rep: 4 (over x).
Axes of the slice: x: 4, y: 8, z: 8, core: 2. Of those that a mesh axis runs over, the one named last changes fastest.
Arguments:
- params: float32 [10, 65536], P(None, 'dev'), may hold values from -8 to 6
- moment1: float32 [10, 65536], P(None, 'dev'), may hold values from -0.06 to 0.06
- moment2: float32 [10, 65536], P(None, 'dev'), may hold values from 0.0001 to 0.01
- camera: float32 [4, 8], P('rep'), may hold values from -3 to 3
- owner: int32 [4, 256, 512, 1], P('rep', 'dev'), may hold values from 0 to 127; in each aligned block of 1024 rows (0 to 1023, 1024 to 2047, ..., all dimensions but the last counted through in order) at most 16 rows name the same one
- local_index: int32 [4, 256, 512], P('rep', 'dev'), may hold values from 0 to 511
- target: float32 [4, 256, 3, 256], P('rep', 'dev'), may hold values from 0 to 1
- rehome: int32 [128, 128], P('dev'), may hold values from 0 to 127, each once within a row
Outputs:
- params_next: float32 [10, 65536], P(None, 'dev')
- moment1_next: float32 [10, 65536], P(None, 'dev')
- moment2_next: float32 [10, 65536], P(None, 'dev')
- rendered: float32 [4, 256, 3, 256], P('rep', 'dev')
The draws below stay inside these ranges and needn't reach their ends.
Inputs may be any that keep to these rules, and one draw needn't show every extreme that they name: In the entries of one device's tiles of one camera (aligned blocks of 1024 entries) no owner is named more than 16 times, a bound that some block reaches. `rehome`: each row is a permutation of the devices.
All inputs are finite; a program needn't handle non-finite values.
Results may differ from the reference program's by a relative error of at most 0.00014.
Values sent between devices are 32-bit elements; how exact they have to be, the bound alone decides.
No kernel may reach another device: no remote copies, remote signals or barrier semaphores. Data moves between devices by JAX's collectives and lax.ppermute only.
A program may use at most 128 MiB of HBM per device.

```python
import math
import jax
import jax.numpy as jnp
import numpy as np
from jax import lax

SIDE = 16
PIX = 256
K = 512
G_DEV = 512
TILE_DEV = 2
GAUSS = 65536
TILES = 256
CAP = 16
SUB = 4
N_DEV = 128
N_REP = 4


def draw_params(key, part):
    keys = jax.random.split(jax.random.fold_in(key, 17), 5)
    scale_lo, scale_hi, opac_lo, opac_hi = (-4.0, -1.0, -7.0, -3.0)
    means = jax.random.uniform(keys[0], (3, GAUSS), jnp.float32, -6.0, 6.0)
    log_scales = jax.random.uniform(keys[1], (2, GAUSS), jnp.float32, scale_lo, scale_hi)
    skewness = jax.random.uniform(keys[2], (1, GAUSS), jnp.float32, -2.0, 2.0)
    opacity = jax.random.uniform(keys[3], (1, GAUSS), jnp.float32, opac_lo, opac_hi)
    colors = jax.random.uniform(keys[4], (3, GAUSS), jnp.float32, -3.0, 3.0)
    return jnp.concatenate([means, log_scales[0:1], skewness, log_scales[1:2], opacity, colors], axis=0)


def plant(result, own_key, smallest, high):
    longest = result.shape.index(max(result.shape))
    spots = []
    for shift in (0, 1):
        where = [jax.random.randint(jax.random.fold_in(own_key, axis), (), 0, length) for axis, length in enumerate(result.shape)]
        where[longest] = (where[longest] + shift) % result.shape[longest]
        spots.append(tuple(where))
    return result.at[spots[0]].set(smallest).at[spots[1]].set(high)


def block_scale(stream_key, extent, shards, low, largest):
    gain = 1.0
    for position, shards_of in shards:
        steps = jax.random.uniform(jax.random.fold_in(jax.random.fold_in(stream_key, 6), position), (shards_of,), jnp.float32, low / len(shards), largest / len(shards))
        gain = gain * jnp.repeat(jnp.exp(steps), extent[position] // shards_of).reshape((-1,) + (1,) * (len(extent) - 1 - position))
    return gain


def routed_block(rng, own, number, rows, number_of, top, reach, slope):
    ranking = jax.random.permutation(rng, number_of)
    crowded, usual = shares(number_of, rows * top, reach, slope, True), shares(number_of, rows * top, reach, slope, False)
    places = jnp.arange(number_of)

    def named(lengths, offset_by):
        used = int((lengths > 0).sum())
        fixed = max(1, used // 4)
        shifted = fixed + (places - fixed + offset_by * (used - fixed)) % max(1, number_of - fixed)
        return jnp.zeros((number_of,), jnp.int32).at[ranking[jnp.where(places < fixed, places, shifted)]].set(jnp.asarray(lengths, jnp.int32))

    lengths = jnp.where(number % 4 == 0, named(crowded, number // 4), named(usual, number - number // 4 - 1))
    mixed = jax.random.permutation(jax.random.fold_in(own, 3), number_of)
    giver, taker = mixed[0:number_of // 2 * 2:2], mixed[1:number_of // 2 * 2:2]
    room = jnp.minimum(lengths[giver] - 1, reach - lengths[taker]) // 2
    room = jnp.where((giver == ranking[0]) | (taker == ranking[0]) | (lengths[taker] == 0), 0, jnp.maximum(room, 0))
    shifted = jax.random.randint(jax.random.fold_in(own, 4), (number_of // 2,), 0, 1 << 20) % (room + 1)
    lengths = lengths.at[giver].add(-shifted).at[taker].add(shifted)
    items = jnp.searchsorted(jnp.cumsum(lengths), jnp.arange(rows * top), side="right").astype(jnp.int32)
    grid = items.reshape(top, rows).T
    grid = grid[jax.random.permutation(jax.random.fold_in(own, 1), rows)]
    offset_by = jax.random.randint(jax.random.fold_in(own, 2), (rows, 1), 0, top)
    return jnp.take_along_axis(grid, (jnp.arange(top)[None, :] + offset_by) % top, axis=1)


def shares(number_of, total, reach, slope, full):
    weights = [(1 << 20) // math.isqrt(standing ** slope) + 1 for standing in range(1, number_of + 1)]
    largest = reach if full else min(reach, max(-(-total // number_of), total * weights[0] // sum(weights)))
    least = 1 if total - largest >= number_of - 1 else 0
    given, spare = [largest] + [least] * (number_of - 1), total - largest - least * (number_of - 1)
    while spare > 0:
        movable = [i for i in range(1, number_of) if given[i] < largest] or [i for i in range(1, number_of) if given[i] < reach]
        whole, budget = sum([weights[i] for i in movable]), spare
        for i in movable:
            addition = min(reach - given[i], max(1, budget * weights[i] // whole), spare)
            given[i] = given[i] + addition
            spare = spare - addition
    return np.array(given)


def gaussian(own_key, extent, scale, limit, pieces=(), dtype=jnp.bfloat16):
    values = jax.random.normal(own_key, extent, jnp.float32) * scale
    if len(pieces) > 0:
        values = block_scale(own_key, extent, pieces, -0.22, 0.18) * values
    return jnp.clip(values, min=-limit, max=limit).astype(dtype)


def setup_inputs(seed: int = 0) -> dict:
    seeds = jax.random.split(jax.random.key(seed), 9)
    params = draw_params(jax.random.fold_in(seeds[8], 71), 0)
    moment1 = gaussian(seeds[1], (10, GAUSS), 0.01, 0.06, ((1, 128),), jnp.float32)
    moment2 = jnp.clip(jnp.exp(math.log(0.01) - 4.6051702 * jax.random.uniform(seeds[2], (10, GAUSS), jnp.float32) ** block_scale(seeds[2], (10, GAUSS), ((1, 128),), -0.2, 0.2)), 0.0001, 0.01)
    camera = gaussian(seeds[3], (N_REP, 8), 1.0, 3.0, ((0, 4),), jnp.float32)
    owner_keys = jax.random.split(jax.random.fold_in(seeds[4], 1), N_REP * TILES * K // (TILE_DEV * K))
    owner_turns = jax.random.permutation(jax.random.fold_in(seeds[4], 3), N_REP * TILES * K // (TILE_DEV * K))
    owner = jax.vmap(lambda own, number: routed_block(jax.random.fold_in(seeds[4], 2), own, number, TILE_DEV * K, N_DEV, 1, CAP, 1))(owner_keys, owner_turns).reshape((N_REP, TILES, K, 1))
    local_index = plant(jax.random.randint(seeds[5], (N_REP, TILES, K), 0, G_DEV), jax.random.fold_in(seeds[5], 1), 0, G_DEV - 1).astype(jnp.int32)
    target = jnp.clip(1.0 * jax.random.uniform(seeds[6], (N_REP, TILES, 3, PIX), jnp.float32) ** block_scale(seeds[6], (N_REP, TILES, 3, PIX), ((0, 4), (1, 128)), -0.2, 0.2), 0.0, 1.0)
    rehome = jax.vmap(lambda own: jax.random.permutation(own, N_DEV))(jax.random.split(seeds[7], N_DEV)).reshape((N_DEV, N_DEV)).astype(jnp.int32)
    return {"params": params, "moment1": moment1, "moment2": moment2, "camera": camera, "owner": owner, "local_index": local_index, "target": target, "rehome": rehome}


BACKGROUND = 0.5

def project(params, camera_row):
    xpos = params[0]
    ypos = params[1]
    zpos = params[2]
    screen_u = camera_row[0] * xpos + camera_row[1] * ypos + camera_row[2] * zpos + camera_row[3]
    screen_v = camera_row[4] * xpos + camera_row[5] * ypos + camera_row[6] * zpos + camera_row[7]
    conic_a = jnp.exp(params[3])
    conic_c = jnp.exp(params[5])
    conic_b = 0.9 * jnp.tanh(params[4]) * jnp.sqrt(conic_a * conic_c)
    opacity = jax.nn.sigmoid(params[6])
    colors = jax.nn.sigmoid(params[7:10])
    head = jnp.stack([screen_u, screen_v, conic_a, conic_b, conic_c, opacity])
    return jnp.concatenate([head, colors], axis=0)

def render(values):
    pixel_ids = jnp.arange(PIX)
    column = (pixel_ids % SIDE).astype(jnp.float32) - 7.5
    row_pos = (pixel_ids // SIDE).astype(jnp.float32) - 7.5
    delta_u = column[None, :, None] - values[:, 0][:, None, :]
    delta_v = row_pos[None, :, None] - values[:, 1][:, None, :]
    quad = values[:, 2][:, None, :] * delta_u * delta_u + 2.0 * values[:, 3][:, None, :] * delta_u * delta_v + values[:, 4][:, None, :] * delta_v * delta_v
    alpha = 0.99 * values[:, 5][:, None, :] * jnp.exp(-0.5 * quad)
    log_keep = jnp.log(1.0 - alpha)
    running = jnp.cumsum(log_keep, axis=2)
    weight = alpha * jnp.exp(running - log_keep)
    image = jnp.einsum('bpk,bck->bcp', weight, values[:, 6:9], precision=lax.Precision.HIGHEST)
    return image + BACKGROUND * jnp.exp(running[:, :, -1])[:, None, :]

def rehome_array(array, inverse):
    blocks = array.reshape(10, N_DEV, N_DEV, SUB)
    moved = jnp.take_along_axis(blocks, inverse[None, :, :, None], axis=2)
    return moved.transpose(0, 2, 1, 3).reshape(10, GAUSS)

def reference(params, moment1, moment2, camera, owner, local_index, target, rehome):
    global_ids = owner[..., 0] * G_DEV + local_index
    grad_total = jnp.zeros_like(params)
    images = []
    for replica in range(N_REP):
        camera_row = camera[replica]

        def project_one(table_params):
            return project(table_params, camera_row)
        projected, pullback = jax.vjp(project_one, params)
        id_blocks = global_ids[replica].reshape(-1, 2, K)
        target_blocks = target[replica].reshape(-1, 2, 3, PIX)

        def total_loss(table):

            def one_block(pair):
                block_ids, block_target = pair
                values = jnp.take(table, block_ids.reshape(-1), axis=1).reshape(9, 2, K).transpose(1, 0, 2)
                image = render(values)
                return (image, 0.5 * jnp.sum((image - block_target) ** 2))
            shown, losses = lax.map(jax.checkpoint(one_block), (id_blocks, target_blocks))
            return (jnp.sum(losses), shown)
        (unused_loss, shown), grad_table = jax.value_and_grad(total_loss, has_aux=True)(projected)
        grad_total = grad_total + pullback(grad_table)[0]
        images.append(shown.reshape(TILES, 3, PIX))
    moment1_new = 0.9 * moment1 + 0.1 * grad_total
    moment2_new = 0.99 * moment2 + 0.01 * grad_total * grad_total
    params_new = params - 0.01 * moment1_new / (jnp.sqrt(moment2_new) + 1e-08)
    inverse = jnp.argsort(rehome, axis=1).astype(jnp.int32)
    return (rehome_array(params_new, inverse), rehome_array(moment1_new, inverse), rehome_array(moment2_new, inverse), jnp.stack(images))
```

```python
import functools

import jax
import jax.numpy as jnp
from jax import lax
from jax.experimental import pallas as pl
from jax.experimental.pallas import tpu as pltpu
from jax.sharding import PartitionSpec as P

SIDE = 16
BACKGROUND = 0.5
CAP = 16
ROWS = 16
VMEM = 48 * 1024 * 1024
F32 = jnp.float32
BF16 = jnp.bfloat16


def one_hot(condition):
    return jnp.where(condition, 1.0, 0.0).astype(BF16)


def parts(x, count=3):
    out = []
    for _ in range(count):
        piece = x.astype(BF16)
        out.append(piece)
        x = x - piece.astype(F32)
    return out


def iota(shape, dim):
    return lax.broadcasted_iota(jnp.int32, shape, dim)


def dot(a, b):
    return lax.dot_general(a, b, (((1,), (0,)), ((), ())), preferred_element_type=F32)


def dot_t(a, b):
    return lax.dot_general(a, b, (((1,), (1,)), ((), ())), preferred_element_type=F32)


def call(body, out_shape, scratch=(), smem=()):
    def run(*args):
        specs = [
            pl.BlockSpec(memory_space=pltpu.SMEM if i in smem else pltpu.VMEM)
            for i in range(len(args))
        ]
        outs = jax.tree.map(lambda _: pl.BlockSpec(memory_space=pltpu.VMEM), out_shape)
        return pl.pallas_call(
            body,
            out_shape=out_shape,
            in_specs=specs,
            out_specs=outs,
            scratch_shapes=list(scratch),
            compiler_params=pltpu.CompilerParams(vmem_limit_bytes=VMEM),
        )(*args)

    return run


def request_body(owner_ref, index_ref, request_ref, rank_ref):
    entries = owner_ref.shape[1]
    devices = request_ref.shape[0]
    step = 256
    before = one_hot(iota((step, step), 0) < iota((step, step), 1))
    base = jnp.zeros((devices, 1), F32)
    total = jnp.zeros((devices, 2 * CAP), F32)
    for start in range(0, entries, step):
        owner = owner_ref[:, start : start + step]
        ids = index_ref[:, start : start + step]
        named = jnp.where(iota((devices, step), 0) == owner, 1.0, 0.0)
        named_b = named.astype(BF16)
        count = dot(named_b, before) + base
        base = base + jnp.sum(named, axis=1, keepdims=True)
        rank = jnp.sum(named * count, axis=0, keepdims=True).astype(jnp.int32)
        rank_ref[:, start : start + step] = rank
        slot = iota((CAP, step), 0) == rank
        high = jnp.where(slot, (ids >> 4).astype(F32), 0.0)
        low = jnp.where(slot, (ids & 15).astype(F32), 0.0)
        total = total + dot_t(named_b, jnp.concatenate([high, low], axis=0).astype(BF16))
    ids = 16.0 * total[:, :CAP] + total[:, CAP:]
    request_ref[...] = jnp.concatenate(
        [ids, jnp.zeros((devices, request_ref.shape[1] - CAP), F32)], axis=1
    )


def asked_hot(request_ref, gauss):
    devices = request_ref.shape[0]
    ids = jnp.transpose(request_ref[...]).astype(jnp.int32)
    return jnp.concatenate(
        [one_hot(iota((gauss, devices), 0) == ids[j : j + 1]) for j in range(CAP)], axis=1
    )


def conics(params_ref):
    conic_a = jnp.exp(params_ref[3:4])
    conic_c = jnp.exp(params_ref[5:6])
    skew = jnp.tanh(params_ref[4:5])
    return conic_a, conic_c, skew, jnp.sqrt(conic_a * conic_c)


def sigmoid(x):
    return 1.0 / (1.0 + jnp.exp(-x))


def respond_body(request_ref, params_ref, camera_ref, response_ref, table):
    gauss = params_ref.shape[1]
    devices = request_ref.shape[0]
    cam = [camera_ref[0, i] for i in range(8)]
    x, y, z = params_ref[0:1], params_ref[1:2], params_ref[2:3]
    conic_a, conic_c, skew, root = conics(params_ref)
    table[...] = jnp.zeros_like(table)
    table[0:1] = cam[0] * x + cam[1] * y + cam[2] * z + cam[3]
    table[1:2] = cam[4] * x + cam[5] * y + cam[6] * z + cam[7]
    table[2:3] = conic_a
    table[3:4] = 0.9 * skew * root
    table[4:5] = conic_c
    table[5:9] = sigmoid(params_ref[6:10])
    hot = asked_hot(request_ref, gauss)
    got = dot(jnp.concatenate(parts(table[...]), axis=0), hot)
    got = got[:ROWS] + got[ROWS : 2 * ROWS] + got[2 * ROWS :]
    for half in range(2):
        block = jnp.concatenate(
            [got[:, j * devices : (j + 1) * devices] for j in range(half * 8, half * 8 + 8)],
            axis=0,
        )
        response_ref[:, half * 128 : half * 128 + 128] = jnp.transpose(block)


def composite_body(
    response_ref, owner_ref, rank_ref, target_ref, image_ref, grad_ref,
    alpha_s, run_s, weight_s, split_s, goal_s, image_s, tail_s, entry_s,
):
    devices = response_ref.shape[0]
    entries = owner_ref.shape[1]
    tiles, _, pix = target_ref.shape
    depth = entries // tiles
    owner, rank = owner_ref[...], rank_ref[...]
    named = one_hot(iota((devices, entries), 0) == owner)
    got = jnp.concatenate(
        [jnp.transpose(response_ref[:, :128]), jnp.transpose(response_ref[:, 128:])], axis=0
    )
    spread = sum(dot(piece, named) for piece in parts(got))
    values = jnp.zeros((ROWS, entries), F32)
    for j in range(CAP):
        values = values + jnp.where(rank == j, spread[j * ROWS : (j + 1) * ROWS], 0.0)
    pad = jnp.zeros((5, pix), F32)
    for t in range(tiles):
        goal_s[t * pix : (t + 1) * pix, 0:8] = jnp.transpose(
            jnp.concatenate([target_ref[t], pad], axis=0)
        )
    rows_of = []
    for t in range(tiles):
        rows_of.append([values[r : r + 1, t * depth : (t + 1) * depth] for r in range(9)])
    across = iota((SIDE, depth), 0).astype(F32) - 7.5

    def chunk(t, i):
        return pl.ds(pl.multiple_of(t * pix + i * SIDE, SIDE), SIDE)

    deltas = []
    for t in range(tiles):
        u, v, conic_a, conic_b, conic_c, opacity = rows_of[t][:6]
        delta_u = across - u
        deltas.append(delta_u)
        first = (-0.5 * conic_a) * delta_u * delta_u
        mixed = -conic_b * delta_u
        half_c = -0.5 * conic_c
        peak = 0.99 * opacity

        def forward(i, carry, t=t, v=v, first=first, mixed=mixed, half_c=half_c, peak=peak):
            delta_v = (i.astype(F32) - 7.5) - v
            power = first + delta_v * (mixed + half_c * delta_v)
            alpha = peak * jnp.exp(power)
            log_keep = jnp.log(1.0 - alpha)
            alpha_s[chunk(t, i)] = alpha
            for n, piece in enumerate(parts(log_keep)):
                split_s[n, chunk(t, i)] = piece
            return carry

        lax.fori_loop(0, pix // SIDE, forward, 0)
    earlier = one_hot(iota((depth, depth), 0) < iota((depth, depth), 1))
    run_s[...] = sum(dot(split_s[n], earlier) for n in range(3))
    color_grads = []
    for t in range(tiles):
        colors = rows_of[t][6:9]

        def shade(i, sums, t=t, colors=colors):
            rows = chunk(t, i)
            alpha = alpha_s[rows]
            through = jnp.exp(run_s[rows])
            weight = alpha * through
            behind = BACKGROUND * through[:, depth - 1 :] * (1.0 - alpha[:, depth - 1 :])
            goal = goal_s[rows]
            slope = jnp.zeros_like(weight)
            out, error = [], jnp.zeros_like(behind)
            for c in range(3):
                shown = jnp.sum(weight * colors[c], axis=1, keepdims=True) + behind
                image_s[rows, c : c + 1] = shown
                gap = shown - goal[:, c : c + 1]
                error = error + gap
                slope = slope + gap * colors[c]
                out.append(sums[c] + gap * weight)
            tail_s[rows, 0:1] = behind * error
            weight_s[rows] = through * slope
            for n, piece in enumerate(parts(weight * slope)):
                split_s[n, rows] = piece
            return tuple(out)

        zero = jnp.zeros((SIDE, depth), F32)
        color_grads.append(lax.fori_loop(0, pix // SIDE, shade, (zero, zero, zero)))
    later = one_hot(iota((depth, depth), 0) > iota((depth, depth), 1))
    run_s[...] = sum(dot(split_s[n], later) for n in range(3))
    entry_s[...] = jnp.zeros_like(entry_s)
    for t in range(tiles):
        u, v, conic_a, conic_b, conic_c, opacity = rows_of[t][:6]
        delta_u = deltas[t]

        def backward(i, sums, t=t, v=v):
            rows = chunk(t, i)
            alpha = alpha_s[rows]
            slope = weight_s[rows] - (run_s[rows] + tail_s[rows, 0:1]) / (1.0 - alpha)
            pull = alpha * slope
            delta_v = (i.astype(F32) - 7.5) - v
            pull_v = pull * delta_v
            return sums[0] + pull, sums[1] + pull_v, sums[2] + pull_v * delta_v

        zero = jnp.zeros((SIDE, depth), F32)
        plain, with_v, with_vv = lax.fori_loop(0, pix // SIDE, backward, (zero, zero, zero))

        def over(a):
            return jnp.sum(a, axis=0, keepdims=True)

        s_u, s_v = over(plain * delta_u), over(with_v)
        cols = slice(t * depth, (t + 1) * depth)
        entry_s[0:1, cols] = conic_a * s_u + conic_b * s_v
        entry_s[1:2, cols] = conic_b * s_u + conic_c * s_v
        entry_s[2:3, cols] = -0.5 * over(plain * delta_u * delta_u)
        entry_s[3:4, cols] = -over(with_v * delta_u)
        entry_s[4:5, cols] = -0.5 * over(with_vv)
        entry_s[5:6, cols] = over(plain) / opacity
        for c in range(3):
            entry_s[6 + c : 7 + c, cols] = over(color_grads[t][c])
        image_ref[t] = jnp.transpose(image_s[t * pix : (t + 1) * pix, 0:8])[0:3]
    grads = entry_s[...]
    slots = jnp.concatenate([jnp.where(rank == j, grads, 0.0) for j in range(CAP)], axis=0)
    sent = sum(dot_t(piece, named) for piece in parts(slots))
    grad_ref[:, :128] = jnp.transpose(sent[:128])
    grad_ref[:, 128:] = jnp.transpose(sent[128:])


def pullback_body(grad_ref, request_ref, params_ref, camera_ref, out_ref):
    gauss = params_ref.shape[1]
    cam = [camera_ref[0, i] for i in range(8)]
    hot = asked_hot(request_ref, gauss)
    came = jnp.concatenate(
        [jnp.transpose(grad_ref[:, :128]), jnp.transpose(grad_ref[:, 128:])], axis=0
    )
    came = jnp.concatenate([came[j * ROWS : (j + 1) * ROWS] for j in range(CAP)], axis=1)
    total = dot_t(jnp.concatenate(parts(came), axis=0), hot)
    total = total[:ROWS] + total[ROWS : 2 * ROWS] + total[2 * ROWS :]
    g_u, g_v, g_a, g_b, g_c = [total[r : r + 1] for r in range(5)]
    conic_a, conic_c, skew, root = conics(params_ref)
    half_b = g_b * (0.45 * skew * root)
    out_ref[0:1] = cam[0] * g_u + cam[4] * g_v
    out_ref[1:2] = cam[1] * g_u + cam[5] * g_v
    out_ref[2:3] = cam[2] * g_u + cam[6] * g_v
    out_ref[3:4] = g_a * conic_a + half_b
    out_ref[4:5] = g_b * 0.9 * (1.0 - skew * skew) * root
    out_ref[5:6] = g_c * conic_c + half_b
    level = sigmoid(params_ref[6:10])
    out_ref[6:10] = total[5:9] * level * (1.0 - level)


def adam_body(grads_ref, params_ref, moment1_ref, moment2_ref, rehome_ref, out_ref, stack_s):
    gauss = params_ref.shape[1]
    devices = out_ref.shape[0]
    sub = gauss // devices
    grad = (grads_ref[0] + grads_ref[1]) + (grads_ref[2] + grads_ref[3])
    moment1 = 0.9 * moment1_ref[...] + 0.1 * grad
    moment2 = 0.99 * moment2_ref[...] + 0.01 * grad * grad
    stack_s[...] = jnp.zeros_like(stack_s)
    stack_s[0:10] = params_ref[...] - 0.01 * moment1 / (jnp.sqrt(moment2) + 1e-08)
    stack_s[10:20] = moment1
    stack_s[20:30] = moment2
    block_of = iota((devices, gauss), 1) // sub == iota((devices, gauss), 0)
    homes = jnp.broadcast_to(rehome_ref[...].astype(F32), (8, devices)).astype(BF16)
    homes = dot(homes, one_hot(block_of))[0:1].astype(jnp.int32)
    place = iota((devices, gauss), 0) == homes
    within = iota((devices, gauss), 1) % sub
    pick = jnp.concatenate([one_hot(place & (within == i)) for i in range(sub)], axis=0)
    moved = dot_t(jnp.concatenate(parts(stack_s[...]), axis=0), pick)
    moved = moved[:32] + moved[32:64] + moved[64:]
    moved = jnp.concatenate(
        [moved[:, i * devices : (i + 1) * devices] for i in range(sub)], axis=0
    )
    out_ref[...] = jnp.transpose(moved)


def place_body(came_ref, params_ref, moment1_ref, moment2_ref):
    gauss = params_ref.shape[1]
    devices = came_ref.shape[0]
    sub = gauss // devices
    came = jnp.transpose(came_ref[...])
    came = jnp.concatenate([came[i * 32 : (i + 1) * 32] for i in range(sub)], axis=1)
    row = iota((gauss, gauss), 0)
    spot = one_hot(row % devices * sub + row // devices == iota((gauss, gauss), 1))
    out = dot(jnp.concatenate(parts(came), axis=0), spot)
    out = out[:32] + out[32:64] + out[64:]
    params_ref[...] = out[0:10]
    moment1_ref[...] = out[10:20]
    moment2_ref[...] = out[20:30]


def shape(*dims, dtype=F32):
    return jax.ShapeDtypeStruct(dims, dtype)


def exchange(x, axis="dev"):
    devices = lax.axis_size(axis)
    parcel = x.reshape(devices, -1, 128)
    return lax.all_to_all(parcel, axis, 0, 0, tiled=True).reshape(x.shape)


def local(params, moment1, moment2, camera, owner, local_index, target, rehome):
    devices = lax.axis_size("dev")
    reps = lax.axis_size("rep")
    gauss = params.shape[1]
    _, tiles, depth = local_index.shape
    entries = tiles * depth
    pix = target.shape[3]
    owners = owner.reshape(1, entries)
    ids = local_index.reshape(1, entries)
    request, rank = call(
        request_body, (shape(devices, 128), shape(1, entries, dtype=jnp.int32))
    )(owners, ids)
    request = exchange(request)
    response = call(
        respond_body, shape(devices, 256), [pltpu.VMEM((ROWS, gauss), F32)], smem=(2,)
    )(request, params, camera)
    response = exchange(response)
    plane = pltpu.VMEM((tiles * pix, depth), F32)
    column = pltpu.VMEM((tiles * pix, 128), F32)
    images, grads = call(
        composite_body,
        (shape(tiles, 3, pix), shape(devices, 256)),
        [
            plane, plane, plane, pltpu.VMEM((3, tiles * pix, depth), BF16),
            column, column, column, pltpu.VMEM((ROWS, entries), F32),
        ],
    )(response, owners, rank, target[0])
    grads = exchange(grads)
    grads = call(pullback_body, shape(10, gauss), smem=(3,))(grads, request, params, camera)
    grads = lax.all_to_all(
        jnp.broadcast_to(grads[None], (reps, 10, gauss)), "rep", 0, 0, tiled=True
    )
    moved = call(adam_body, shape(devices, 128), [pltpu.VMEM((32, gauss), F32)])(
        grads, params, moment1, moment2, rehome
    )
    moved = exchange(moved)
    out = call(place_body, (shape(10, gauss),) * 3)(moved)
    return (*out, images[None])


def solution(mesh):
    in_specs = (
        P(None, "dev"),
        P(None, "dev"),
        P(None, "dev"),
        P("rep", None),
        P("rep", "dev", None, None),
        P("rep", "dev", None),
        P("rep", "dev", None, None),
        P("dev", None),
    )
    out_specs = (P(None, "dev"), P(None, "dev"), P(None, "dev"), P("rep", "dev", None, None))
    return jax.shard_map(local, mesh=mesh, in_specs=in_specs, out_specs=out_specs, check_vma=False)
```

```python
import functools

import jax
import jax.numpy as jnp
from jax import lax
from jax.experimental import pallas as pl
from jax.experimental.pallas import tpu as pltpu
from jax.sharding import PartitionSpec as P

SIDE = 16
BACKGROUND = 0.5
CAP = 16
SUB = 4
HOME_CAP = 32
UNROLL = 4
ROWS = 16
VMEM = 48 * 1024 * 1024
F32 = jnp.float32
BF16 = jnp.bfloat16


def one_hot(condition):
    return jnp.where(condition, 1.0, 0.0).astype(BF16)


def parts(x, count=3):
    out = []
    for _ in range(count):
        piece = x.astype(BF16)
        out.append(piece)
        x = x - piece.astype(F32)
    return out


def iota(shape, dim):
    return lax.broadcasted_iota(jnp.int32, shape, dim)


def dot(a, b):
    return lax.dot_general(a, b, (((1,), (0,)), ((), ())), preferred_element_type=F32)


def dot_t(a, b):
    return lax.dot_general(a, b, (((1,), (1,)), ((), ())), preferred_element_type=F32)


def call(body, out_shape, scratch=(), smem=()):
    def run(*args):
        specs = [
            pl.BlockSpec(memory_space=pltpu.SMEM if i in smem else pltpu.VMEM)
            for i in range(len(args))
        ]
        outs = jax.tree.map(lambda _: pl.BlockSpec(memory_space=pltpu.VMEM), out_shape)
        return pl.pallas_call(
            body,
            out_shape=out_shape,
            in_specs=specs,
            out_specs=outs,
            scratch_shapes=list(scratch),
            compiler_params=pltpu.CompilerParams(vmem_limit_bytes=VMEM),
        )(*args)

    return run


def along(ref):
    return jnp.concatenate([ref[t : t + 1] for t in range(ref.shape[0])], axis=1)


def rank_of(device, devices):
    entries = device.shape[1]
    step = 256
    before = one_hot(iota((step, step), 0) < iota((step, step), 1))
    base = jnp.zeros((devices, 1), F32)
    ranks, hots = [], []
    for start in range(0, entries, step):
        named = jnp.where(
            iota((devices, step), 0) == device[:, start : start + step], 1.0, 0.0
        )
        hots.append(named.astype(BF16))
        count = dot(hots[-1], before) + base
        base = base + jnp.sum(named, axis=1, keepdims=True)
        ranks.append(jnp.sum(named * count, axis=0, keepdims=True).astype(jnp.int32))
    return jnp.concatenate(ranks, axis=1), jnp.concatenate(hots, axis=1)


def homes_of(rehome_ref, gauss):
    devices = rehome_ref.shape[1]
    sub = gauss // devices
    homes = jnp.broadcast_to(rehome_ref[...].astype(F32), (8, devices)).astype(BF16)
    return dot(homes, one_hot(iota((devices, gauss), 1) // sub == iota((devices, gauss), 0)))[0:1]


def pack_blocks(stack, homes, devices):
    gauss = stack.shape[1]
    sub = gauss // devices
    place = iota((devices, gauss), 0) == homes.astype(jnp.int32)
    within = iota((devices, gauss), 1) % sub
    pick = jnp.concatenate([one_hot(place & (within == i)) for i in range(sub)], axis=0)
    moved = dot_t(jnp.concatenate(parts(stack), axis=0), pick)
    moved = moved[:32] + moved[32:64] + moved[64:]
    return jnp.transpose(
        jnp.concatenate([moved[:, i * devices : (i + 1) * devices] for i in range(sub)], axis=0)
    )


def place_blocks(came, gauss):
    devices = came.shape[0]
    sub = gauss // devices
    came = jnp.transpose(came)
    came = jnp.concatenate([came[i * 32 : (i + 1) * 32] for i in range(sub)], axis=1)
    row = iota((gauss, gauss), 0)
    spot = one_hot(row % devices * sub + row // devices == iota((gauss, gauss), 1))
    out = dot(jnp.concatenate(parts(came), axis=0), spot)
    return out[:32] + out[32:64] + out[64:]


def request_body(
    owner_ref, index_ref, params_ref, moment1_ref, moment2_ref, rehome_ref,
    request_ref, rank_ref, stack_s,
):
    gauss = params_ref.shape[1]
    devices = request_ref.shape[0]
    rank, named = rank_of(owner_ref[...], devices)
    rank_ref[...] = rank
    ids = along(index_ref)
    slot = iota((CAP, ids.shape[1]), 0) == rank
    high = jnp.where(slot, (ids >> 4).astype(F32), 0.0)
    low = jnp.where(slot, (ids & 15).astype(F32), 0.0)
    total = dot_t(named, jnp.concatenate([high, low], axis=0).astype(BF16))
    ids = 16.0 * total[:, :CAP] + total[:, CAP:]
    stack_s[...] = jnp.zeros_like(stack_s)
    stack_s[0:10] = params_ref[...]
    stack_s[10:20] = moment1_ref[...]
    stack_s[20:30] = moment2_ref[...]
    request_ref[:, 0:128] = pack_blocks(stack_s[...], homes_of(rehome_ref, gauss), devices)
    request_ref[:, 128:256] = jnp.concatenate([ids, jnp.zeros((devices, 128 - CAP), F32)], axis=1)


def asked_hot(request_ref, gauss):
    devices = request_ref.shape[0]
    ids = jnp.transpose(request_ref[:, 128:256]).astype(jnp.int32)
    return jnp.concatenate(
        [one_hot(iota((gauss, devices), 0) == ids[j : j + 1]) for j in range(CAP)], axis=1
    )


def respond_body(request_ref, params_ref, rehome_ref, response_ref, table):
    gauss = params_ref.shape[1]
    devices = request_ref.shape[0]
    table[...] = jnp.zeros_like(table)
    table[0:10] = params_ref[...]
    table[10:11] = homes_of(rehome_ref, gauss)
    got = dot(jnp.concatenate(parts(table[...]), axis=0), asked_hot(request_ref, gauss))
    got = got[:ROWS] + got[ROWS : 2 * ROWS] + got[2 * ROWS :]
    for half in range(2):
        block = jnp.concatenate(
            [got[:, j * devices : (j + 1) * devices] for j in range(half * 8, half * 8 + 8)],
            axis=0,
        )
        response_ref[:, half * 128 : half * 128 + 128] = jnp.transpose(block)


def sigmoid(x):
    return 1.0 / (1.0 + jnp.exp(-x))


def stacked(pieces):
    rows = [piece.astype(F32) for piece in pieces]
    return jnp.concatenate([*rows, jnp.zeros_like(rows[0])], axis=0).astype(BF16)


def groups(x):
    return x[0:8] + x[8:16] + x[16:24]


def composite_body(
    response_ref, owner_ref, index_ref, rank_ref, target_ref, camera_ref,
    image_ref, grad_ref, entry_ref,
    alpha_s, run_s, slope_s, split_s, entry_s,
):
    devices = response_ref.shape[0]
    entries = owner_ref.shape[1]
    _, tiles, pix = target_ref.shape
    depth = entries // tiles
    cam = [camera_ref[0, i] for i in range(8)]
    owner, rank = owner_ref[...], rank_ref[...]
    named = one_hot(iota((devices, entries), 0) == owner)
    got = jnp.concatenate(
        [jnp.transpose(response_ref[:, :128]), jnp.transpose(response_ref[:, 128:])], axis=0
    )
    spread = sum(dot(piece, named) for piece in parts(got))
    values = jnp.zeros((ROWS, entries), F32)
    for j in range(CAP):
        values = values + jnp.where(rank == j, spread[j * ROWS : (j + 1) * ROWS], 0.0)
    x, y, z = values[0:1], values[1:2], values[2:3]
    screen_u = cam[0] * x + cam[1] * y + cam[2] * z + cam[3]
    screen_v = cam[4] * x + cam[5] * y + cam[6] * z + cam[7]
    conic_a, conic_c, skew = jnp.exp(values[3:4]), jnp.exp(values[5:6]), jnp.tanh(values[4:5])
    root = jnp.sqrt(conic_a * conic_c)
    conic_b = 0.9 * skew * root
    level = sigmoid(values[0:16])
    opacity = level[6:7]
    entry_s[...] = jnp.zeros_like(entry_s)
    entry_s[0:3] = level[7:10]
    colors = entry_s[0:8]
    peak, half_a, half_c = 0.99 * opacity, -0.5 * conic_a, -0.5 * conic_c
    across = iota((SIDE, depth), 0).astype(F32) - 7.5

    def chunk(t, i):
        return pl.ds(pl.multiple_of(t * pix + i * SIDE, SIDE), SIDE)

    def of(t):
        return slice(t * depth, (t + 1) * depth)

    def over_rows(body, init, t):
        return lax.fori_loop(0, pix // SIDE, functools.partial(body, t), init, unroll=UNROLL)

    def save(rows, x):
        for n, piece in enumerate(parts(x, 2)):
            split_s[n, rows] = piece

    for t in range(tiles):
        delta_u = across - screen_u[:, of(t)]
        first = half_a[:, of(t)] * delta_u * delta_u
        mixed = -conic_b[:, of(t)] * delta_u

        def forward(t, i, carry, first=first, mixed=mixed):
            rows = chunk(t, i)
            delta_v = (i.astype(F32) - 7.5) - screen_v[:, of(t)]
            power = first + delta_v * (mixed + half_c[:, of(t)] * delta_v)
            alpha = peak[:, of(t)] * jnp.exp(power)
            alpha_s[rows] = alpha
            save(rows, jnp.log(1.0 - alpha))
            return carry

        over_rows(forward, 0, t)
    half = depth // 2
    tri = one_hot(iota((half, half), 0) < iota((half, half), 1))
    full = jnp.ones((half, half), BF16)
    run_s[:, :half] = dot(split_s[0, :, :half], tri) + dot(split_s[1, :, :half], tri)
    run_s[:, half:] = (
        dot(split_s[0, :, half:], tri) + dot(split_s[1, :, half:], tri)
        + dot(split_s[0, :, :half], full) + dot(split_s[1, :, :half], full)
    )
    ones = jnp.ones((16, depth), BF16)
    behind = dot_t(ones, split_s[0]) + dot_t(ones, split_s[1])
    behind = BACKGROUND * jnp.exp(behind[0:1])
    for t in range(tiles):

        def weigh(t, i, carry):
            rows = chunk(t, i)
            through = jnp.exp(run_s[rows])
            run_s[rows] = through
            save(rows, alpha_s[rows] * through)
            return carry

        over_rows(weigh, 0, t)
    color_grads, tails = [], []
    for t in range(tiles):
        px = slice(t * pix, (t + 1) * pix)
        paints = parts(colors[:, of(t)])
        paint = stacked(paints)
        shown = groups(dot_t(paint, split_s[0, px]) + dot_t(paint, split_s[1, px]))
        shown = shown + behind[:, px]
        gaps = []
        for c in range(3):
            image_ref[c, t : t + 1] = shown[c : c + 1]
            gaps.append(shown[c : c + 1] - target_ref[c, t : t + 1])
        tail = behind[:, px] * (gaps[0] + gaps[1] + gaps[2])
        gap = jnp.concatenate([*gaps, jnp.zeros((5, pix), F32)], axis=0)
        gap_parts = parts(gap)
        drawn = stacked(gap_parts)
        color_grads.append(groups(dot(drawn, split_s[0, px]) + dot(drawn, split_s[1, px])))
        high, middle, low = [piece.astype(F32) for piece in gap_parts]
        ends = [piece.astype(F32) for piece in parts(tail)]
        ends = jnp.concatenate([*ends, jnp.zeros((5, pix), F32)], axis=0)
        left = jnp.concatenate(
            [high, high, high, middle, middle, low, ends, jnp.zeros((72, pix), F32)], axis=0
        )
        left = jnp.concatenate(
            [jnp.transpose(left[:, :128]), jnp.transpose(left[:, 128:])], axis=0
        ).astype(BF16)
        high, middle, low = [piece.astype(F32) for piece in paints]
        right = jnp.concatenate(
            [high, middle, low, high, middle, high, jnp.zeros((80, depth), F32)], axis=0
        ).astype(BF16)
        slope_s[px] = dot(left, right)
        row = iota((128, depth), 0)
        tails.append(dot(left, one_hot((row >= 48) & (row < 51))))
    for t in range(tiles):

        def spread_back(t, i, carry):
            rows = chunk(t, i)
            through_slope = run_s[rows] * slope_s[rows]
            slope_s[rows] = through_slope
            save(rows, alpha_s[rows] * through_slope)
            return carry

        over_rows(spread_back, 0, t)
    tri = one_hot(iota((half, half), 0) > iota((half, half), 1))
    for t in range(tiles):
        px = slice(t * pix, (t + 1) * pix)
        run_s[px, half:] = (
            dot(split_s[0, px, half:], tri) + dot(split_s[1, px, half:], tri)
            + tails[t][:, half:]
        )
        run_s[px, :half] = (
            dot(split_s[0, px, :half], tri) + dot(split_s[1, px, :half], tri)
            + dot(split_s[0, px, half:], full) + dot(split_s[1, px, half:], full)
            + tails[t][:, :half]
        )
    sums = []
    for t in range(tiles):

        def backward(t, i, sums):
            rows = chunk(t, i)
            alpha = alpha_s[rows]
            pull = alpha * (slope_s[rows] - run_s[rows] / (1.0 - alpha))
            delta_v = (i.astype(F32) - 7.5) - screen_v[:, of(t)]
            pull_v = pull * delta_v
            return sums[0] + pull, sums[1] + pull_v, sums[2] + pull_v * delta_v

        zero = jnp.zeros((SIDE, depth), F32)
        plain, with_v, with_vv = over_rows(backward, (zero, zero, zero), t)
        delta_u = across - screen_u[:, of(t)]
        plain_u = plain * delta_u
        sums.append(
            [
                jnp.sum(a, axis=0, keepdims=True)
                for a in (plain, plain_u, with_v, plain_u * delta_u, with_v * delta_u, with_vv)
            ]
        )
    s_0, s_u, s_v, s_uu, s_uv, s_vv = [
        jnp.concatenate([s[n] for s in sums], axis=1) for n in range(6)
    ]
    g_u = conic_a * s_u + conic_b * s_v
    g_v = conic_b * s_u + conic_c * s_v
    half_b = -0.5 * s_uv * conic_b
    for c in range(3):
        entry_s[c : c + 1] = cam[c] * g_u + cam[4 + c] * g_v
    entry_s[3:4] = half_b - 0.5 * s_uu * conic_a
    entry_s[4:5] = -0.9 * s_uv * (1.0 - skew * skew) * root
    entry_s[5:6] = half_b - 0.5 * s_vv * conic_c
    entry_s[6:7] = s_0 * (1.0 - opacity)
    tint = jnp.concatenate(color_grads, axis=1)[0:3]
    entry_s[7:10] = tint * level[7:10] * (1.0 - level[7:10])
    entry_ref[...] = entry_s[...]
    home = (values[10:11] + 0.5).astype(jnp.int32)
    spot = owner * SUB + along(index_ref) % SUB
    entry_s[10:11] = spot.astype(F32)
    order, moves = rank_of(home, devices)
    slots = iota((HOME_CAP, entries), 0) == order
    grads = entry_s[...]
    sent = 0.0
    for piece in parts(grads, 2):
        piece = piece.astype(F32)
        rows = jnp.concatenate(
            [jnp.where(slots, piece[r : r + 1], 0.0).astype(BF16) for r in range(11)], axis=0
        )
        sent = sent + dot_t(rows, moves)
    over = jnp.max(order, axis=1, keepdims=True) >= HOME_CAP
    flag = jnp.where(over, 1.0, 0.0) + jnp.zeros((HOME_CAP, devices), F32)
    sent = jnp.concatenate([sent, flag], axis=0)
    for n in range(3):
        grad_ref[:, n * 128 : (n + 1) * 128] = jnp.transpose(sent[n * 128 : (n + 1) * 128])


def collect_body(grad_ref, out_ref, came_s):
    gauss = out_ref.shape[1]
    devices = grad_ref.shape[0]
    for n in range(3):
        came_s[n * 128 : (n + 1) * 128] = jnp.transpose(grad_ref[:, n * 128 : (n + 1) * 128])
    spots = (came_s[10 * HOME_CAP : 11 * HOME_CAP] + 0.5).astype(jnp.int32)
    total = jnp.zeros((2 * ROWS, gauss), F32)
    zero = jnp.zeros((6, devices), F32)
    for start in range(0, HOME_CAP, 8):
        hot, came = [], []
        for j in range(start, start + 8):
            hot.append(one_hot(iota((gauss, devices), 0) == spots[j : j + 1]))
            came.append(
                jnp.concatenate([came_s[pl.ds(j, 10, stride=HOME_CAP), :], zero], axis=0)
            )
        came = parts(jnp.concatenate(came, axis=1), 2)
        total = total + dot_t(jnp.concatenate(came, axis=0), jnp.concatenate(hot, axis=1))
    out_ref[...] = total[:ROWS] + total[ROWS:]
    flags = came_s[11 * HOME_CAP : 12 * HOME_CAP]
    flag = jnp.max(jnp.max(flags, axis=1, keepdims=True), axis=0, keepdims=True)
    out_ref[10:11] = flag + jnp.zeros((1, gauss), F32)


def to_owner_body(entry_ref, owner_ref, rank_ref, out_ref):
    devices = out_ref.shape[0]
    rank = rank_ref[...]
    named = one_hot(iota((devices, rank.shape[1]), 0) == owner_ref[...])
    grads = entry_ref[...]
    slots = jnp.concatenate([jnp.where(rank == j, grads, 0.0) for j in range(CAP)], axis=0)
    sent = sum(dot_t(piece, named) for piece in parts(slots))
    out_ref[:, :128] = jnp.transpose(sent[:128])
    out_ref[:, 128:] = jnp.transpose(sent[128:])


def at_owner_body(grad_ref, request_ref, rehome_ref, out_ref, *, gauss):
    devices = grad_ref.shape[0]
    came = jnp.concatenate(
        [jnp.transpose(grad_ref[:, :128]), jnp.transpose(grad_ref[:, 128:])], axis=0
    )
    came = jnp.concatenate([came[j * ROWS : (j + 1) * ROWS] for j in range(CAP)], axis=1)
    total = dot_t(jnp.concatenate(parts(came), axis=0), asked_hot(request_ref, gauss))
    total = total[:ROWS] + total[ROWS : 2 * ROWS] + total[2 * ROWS :]
    stack = jnp.concatenate([total, jnp.zeros_like(total)], axis=0)
    out_ref[...] = pack_blocks(stack, homes_of(rehome_ref, gauss), devices)


def at_home_body(came_ref, out_ref):
    out_ref[...] = place_blocks(came_ref[...], out_ref.shape[1])[:ROWS]


def adam_body(grads_ref, request_ref, params_ref, moment1_ref, moment2_ref):
    old = place_blocks(request_ref[:, 0:128], params_ref.shape[1])
    grad = (grads_ref[0] + grads_ref[1]) + (grads_ref[2] + grads_ref[3])
    grad = grad[0:10]
    moment1 = 0.9 * old[10:20] + 0.1 * grad
    moment2 = 0.99 * old[20:30] + 0.01 * grad * grad
    params_ref[...] = old[0:10] - 0.01 * moment1 / (jnp.sqrt(moment2) + 1e-08)
    moment1_ref[...] = moment1
    moment2_ref[...] = moment2


def shape(*dims, dtype=F32):
    return jax.ShapeDtypeStruct(dims, dtype)


def exchange(x):
    devices = lax.axis_size("dev")
    parcel = x.reshape(devices, -1, 128)
    return lax.all_to_all(parcel, "dev", 0, 0, tiled=True).reshape(x.shape)


def share(x):
    copies = jnp.broadcast_to(x[None], (lax.axis_size("rep"), *x.shape))
    return lax.all_to_all(copies, "rep", 0, 0, tiled=True)


def local(params, moment1, moment2, camera, owner, local_index, target, rehome):
    devices = lax.axis_size("dev")
    gauss = params.shape[1]
    _, tiles, depth = local_index.shape
    entries = tiles * depth
    pix = target.shape[3]
    owners = owner.reshape(1, entries)
    ids = local_index[0]
    request, rank = call(
        request_body,
        (shape(devices, 256), shape(1, entries, dtype=jnp.int32)),
        [pltpu.VMEM((32, gauss), F32)],
    )(owners, ids, params, moment1, moment2, rehome)
    request = exchange(request)
    response = call(respond_body, shape(devices, 256), [pltpu.VMEM((ROWS, gauss), F32)])(
        request, params, rehome
    )
    response = exchange(response)
    plane = pltpu.VMEM((tiles * pix, depth), F32)
    images, grads, by_entry = call(
        composite_body,
        (shape(3, tiles, pix), shape(devices, 384), shape(ROWS, entries)),
        [
            plane, plane, plane, pltpu.VMEM((2, tiles * pix, depth), BF16),
            pltpu.VMEM((ROWS, entries), F32),
        ],
        smem=(5,),
    )(response, owners, ids, rank, target[0].transpose(1, 0, 2), camera)
    grads = exchange(grads)
    grads = call(collect_body, shape(ROWS, gauss), [pltpu.VMEM((384, devices), F32)])(grads)
    grads = share(grads)

    def by_owner(grads, by_entry, owners, rank, request, rehome):
        sent = call(to_owner_body, shape(devices, 256))(by_entry, owners, rank)
        sent = call(functools.partial(at_owner_body, gauss=gauss), shape(devices, 128))(
            exchange(sent), request, rehome
        )
        return share(call(at_home_body, shape(ROWS, gauss))(exchange(sent)))

    full = jnp.max(grads[:, 10, 0]) > 0.5
    grads = lax.cond(
        full, by_owner, lambda grads, *rest: grads, grads, by_entry, owners, rank, request, rehome
    )
    out = call(adam_body, (shape(10, gauss),) * 3)(grads, request)
    return (*out, images.transpose(1, 0, 2)[None])


def solution(mesh):
    in_specs = (
        P(None, "dev"),
        P(None, "dev"),
        P(None, "dev"),
        P("rep", None),
        P("rep", "dev", None, None),
        P("rep", "dev", None),
        P("rep", "dev", None, None),
        P("dev", None),
    )
    out_specs = (P(None, "dev"), P(None, "dev"), P(None, "dev"), P("rep", "dev", None, None))
    return jax.shard_map(local, mesh=mesh, in_specs=in_specs, out_specs=out_specs, check_vma=False)
```

```python
import functools

import jax
import jax.numpy as jnp
from jax import lax
from jax.experimental import pallas as pl
from jax.experimental.pallas import tpu as pltpu
from jax.sharding import PartitionSpec as P

SIDE = 16
BACKGROUND = 0.5
CAP = 16
SUB = 4
HOME_CAP = 25
SENT = 10
VALUES = 10
UNROLL = 16
ROWS = 16
VMEM = 40 * 1024 * 1024
F32 = jnp.float32
BF16 = jnp.bfloat16


def one_hot(condition):
    return jnp.where(condition, 1.0, 0.0).astype(BF16)


def parts(x, count=3):
    out = []
    for _ in range(count):
        piece = x.astype(BF16)
        out.append(piece)
        x = x - piece.astype(F32)
    return out


def iota(shape, dim):
    return lax.broadcasted_iota(jnp.int32, shape, dim)


def dot(a, b):
    return lax.dot_general(a, b, (((1,), (0,)), ((), ())), preferred_element_type=F32)


def dot_t(a, b):
    return lax.dot_general(a, b, (((1,), (1,)), ((), ())), preferred_element_type=F32)


def call(body, out_shape, scratch=(), smem=(), hbm=(), smem_out=(), hbm_out=(), vmem=VMEM):
    def run(*args):
        space = [
            pltpu.SMEM if i in smem else pl.ANY if i in hbm else pltpu.VMEM
            for i in range(len(args))
        ]
        outs = jax.tree.map(lambda _: pl.BlockSpec(memory_space=pltpu.VMEM), out_shape)
        if smem_out or hbm_out:
            outs = tuple(
                pl.BlockSpec(
                    memory_space=pltpu.SMEM if i in smem_out else pl.ANY if i in hbm_out else pltpu.VMEM
                )
                for i in range(len(out_shape))
            )
        return pl.pallas_call(
            body,
            out_shape=out_shape,
            in_specs=[pl.BlockSpec(memory_space=m) for m in space],
            out_specs=outs,
            scratch_shapes=list(scratch),
            compiler_params=pltpu.CompilerParams(vmem_limit_bytes=vmem),
        )(*args)

    return run


def start(source, place, sem):
    copy = pltpu.make_async_copy(source, place, sem)
    copy.start()
    return copy


def along(ref):
    return jnp.concatenate([ref[t : t + 1] for t in range(ref.shape[0])], axis=1)


def rank_of(device, devices):
    entries = device.shape[1]
    step = 256
    before = one_hot(iota((step, step), 0) < iota((step, step), 1))
    base = jnp.zeros((devices, 1), F32)
    ranks, hots = [], []
    for start in range(0, entries, step):
        named = jnp.where(
            iota((devices, step), 0) == device[:, start : start + step], 1.0, 0.0
        )
        hots.append(named.astype(BF16))
        count = dot(hots[-1], before) + base
        base = base + jnp.sum(named, axis=1, keepdims=True)
        ranks.append(jnp.sum(named * count, axis=0, keepdims=True).astype(jnp.int32))
    return jnp.concatenate(ranks, axis=1), jnp.concatenate(hots, axis=1)


def homes_of(rehome_ref, gauss):
    devices = rehome_ref.shape[1]
    sub = gauss // devices
    homes = jnp.broadcast_to(rehome_ref[...].astype(F32), (8, devices)).astype(BF16)
    return dot(homes, one_hot(iota((devices, gauss), 1) // sub == iota((devices, gauss), 0)))[0:1]


def pack_blocks(stack, homes, devices, rows):
    gauss = stack.shape[1]
    sub = gauss // devices
    place = iota((devices, gauss), 0) == homes.astype(jnp.int32)
    within = iota((devices, gauss), 1) % sub
    pick = jnp.concatenate([one_hot(place & (within == i)) for i in range(sub)], axis=0)
    moved = dot_t(jnp.concatenate(parts(stack), axis=0), pick)
    moved = moved[:32] + moved[32:64] + moved[64:]
    moved = [moved[:rows, i * devices : (i + 1) * devices] for i in range(sub)]
    if sub * rows < 128:
        moved.append(jnp.zeros((128 - sub * rows, devices), F32))
    return jnp.transpose(jnp.concatenate(moved, axis=0))[:, : sub * rows]


def place_blocks(blocks, devices):
    sub = len(blocks)
    gauss = sub * devices
    row = iota((gauss, gauss), 0)
    spot = one_hot(row % devices * sub + row // devices == iota((gauss, gauss), 1))
    came = jnp.concatenate(blocks, axis=1)
    out = dot(jnp.concatenate(parts(came), axis=0), spot)
    return out[:32] + out[32:64] + out[64:]


def sigmoid(x):
    return 1.0 / (1.0 + jnp.exp(-x))


def conics(rows):
    conic_a, conic_c, skew = jnp.exp(rows[3:4]), jnp.exp(rows[5:6]), jnp.tanh(rows[4:5])
    return conic_a, conic_c, skew, jnp.sqrt(conic_a * conic_c)


def request_body(
    owner_hbm, index_hbm, moment2_hbm, rehome_hbm,
    request_hbm, lists_hbm,
    owner_s, index_s, moment2_s, rehome_s, stack_s, request_s, lists_s, sems,
):
    copies = [
        start(source, place, sems.at[n])
        for n, (source, place) in enumerate(
            [
                (owner_hbm, owner_s), (index_hbm, index_s),
                (rehome_hbm, rehome_s), (moment2_hbm, moment2_s),
            ]
        )
    ]
    gauss = moment2_s.shape[1]
    devices = request_s.shape[0]
    stack_s[...] = jnp.zeros_like(stack_s)
    lists_s[...] = jnp.zeros_like(lists_s)
    for copy in copies:
        copy.wait()
    owner, ids = owner_s[...], along(index_s)
    rank, named = rank_of(owner, devices)
    homes = homes_of(rehome_s, gauss)
    lists_s[3:4, 0:gauss] = homes.astype(jnp.int32)
    lists_s[0:1] = owner
    lists_s[1:2] = ids
    lists_s[2:3] = rank
    kept = start(lists_s, lists_hbm, sems.at[4])
    slot = iota((CAP, ids.shape[1]), 0) == rank
    high = jnp.where(slot, (ids >> 4).astype(F32), 0.0)
    low = jnp.where(slot, (ids & 15).astype(F32), 0.0)
    total = dot_t(named, jnp.concatenate([high, low], axis=0).astype(BF16))
    asked = 16.0 * total[:, :CAP] + total[:, CAP:]
    stack_s[0:10] = moment2_s[...]
    blocks = pack_blocks(stack_s[...], homes, devices, 16)
    zero = jnp.zeros((devices, 128 - CAP - blocks.shape[1]), F32)
    request_s[...] = jnp.concatenate([blocks, asked, zero], axis=1)
    sent = start(request_s, request_hbm, sems.at[5])
    kept.wait()
    sent.wait()


def table_body(
    params_ref, moment1_ref, camera_ref, lists_ref, target_ref,
    table_ref, blocks_ref, kept_lists_ref, kept_target_ref, stack_s,
):
    kept_lists_ref[...] = lists_ref[...]
    kept_target_ref[...] = target_ref[...]
    gauss = params_ref.shape[1]
    devices = blocks_ref.shape[1]
    cam = [camera_ref[0, i] for i in range(8)]
    homes = lists_ref[3:4, 0:gauss].astype(F32)
    params = params_ref[...]
    stack_s[...] = jnp.zeros_like(stack_s)
    stack_s[0:10] = params
    stack_s[10:20] = moment1_ref[...]
    blocks = pack_blocks(stack_s[...], homes, devices, 24)
    zero = jnp.zeros((devices, 128 - blocks.shape[1]), F32)
    blocks = jnp.transpose(jnp.concatenate([blocks, zero], axis=1))
    blocks_ref[...] = blocks[: blocks_ref.shape[0]]
    x, y, z = params[0:1], params[1:2], params[2:3]
    conic_a, conic_c, skew, root = conics(params)
    table_ref[...] = jnp.zeros_like(table_ref)
    table_ref[0:1] = cam[0] * x + cam[1] * y + cam[2] * z + cam[3]
    table_ref[1:2] = cam[4] * x + cam[5] * y + cam[6] * z + cam[7]
    table_ref[2:3] = conic_a
    table_ref[3:4] = 0.9 * skew * root
    table_ref[4:5] = conic_c
    table_ref[5:9] = sigmoid(params[6:10])
    table_ref[9:10] = homes


def asked_hot(request_ref, gauss):
    devices = request_ref.shape[0]
    ids = jnp.transpose(request_ref[...])[64 : 64 + CAP].astype(jnp.int32)
    return jnp.concatenate(
        [one_hot(iota((gauss, devices), 0) == ids[j : j + 1]) for j in range(CAP)], axis=1
    )


def respond_body(request_ref, table_ref, blocks_ref, response_ref, out_s):
    gauss = table_ref.shape[1]
    devices = request_ref.shape[0]
    got = dot(jnp.concatenate(parts(table_ref[...]), axis=0), asked_hot(request_ref, gauss))
    got = got[:ROWS] + got[ROWS : 2 * ROWS] + got[2 * ROWS :]
    for j in range(CAP):
        out_s[pl.ds(j, VALUES, stride=CAP), :] = got[:VALUES, j * devices : (j + 1) * devices]
    out_s[VALUES * CAP :] = blocks_ref[...]
    response_ref[:, :128] = jnp.transpose(out_s[:128])
    response_ref[:, 128:] = jnp.transpose(out_s[128:])


def settle(request_ref, response_ref, old_ref):
    devices = request_ref.shape[0]
    sub = old_ref.shape[1] // devices
    first = jnp.transpose(request_ref[...])
    second = jnp.transpose(response_ref[:, 128:])[VALUES * CAP - 128 :]
    blocks = [
        jnp.concatenate(
            [second[i * 24 : i * 24 + 24], jnp.zeros((8, devices), F32)], axis=0
        )
        for i in range(sub)
    ]
    old_ref[0:20] = place_blocks(blocks, devices)[0:20]
    blocks = [
        jnp.concatenate([first[i * 16 : i * 16 + 16], jnp.zeros((16, devices), F32)], axis=0)
        for i in range(sub)
    ]
    old_ref[20:30] = place_blocks(blocks, devices)[0:10]
    old_ref[30:32] = jnp.zeros((2, old_ref.shape[1]), F32)


def stacked(pieces):
    rows = [piece.astype(F32) for piece in pieces]
    return jnp.concatenate([*rows, jnp.zeros_like(rows[0])], axis=0).astype(BF16)


def groups(x):
    return x[0:8] + x[8:16] + x[16:24]


def composite_body(
    response_ref, lists_ref, target_ref,
    image_ref, grad_ref, entry_ref,
    alpha_s, run_s, slope_s, split_s, entry_s, sent_s,
):
    devices = response_ref.shape[0]
    entries = lists_ref.shape[1]
    _, tiles, pix = target_ref.shape
    depth = entries // tiles
    owner, ids, rank = lists_ref[0:1], lists_ref[1:2], lists_ref[2:3]
    named = one_hot(iota((devices, entries), 0) == owner)
    got = jnp.concatenate(
        [jnp.transpose(response_ref[:, :128]), jnp.transpose(response_ref[:, 128:])], axis=0
    )[: VALUES * CAP]
    spread = sum(dot(piece, named) for piece in parts(got))
    mine = iota((CAP, entries), 0) == rank
    values = [
        jnp.sum(jnp.where(mine, spread[r * CAP : (r + 1) * CAP], 0.0), axis=0, keepdims=True)
        for r in range(VALUES)
    ]
    screen_u, screen_v, conic_a, conic_b, conic_c, opacity = values[:6]
    entry_s[...] = jnp.zeros_like(entry_s)
    for c in range(3):
        entry_s[c : c + 1] = values[6 + c]
    colors = entry_s[0:8]
    peak, half_a, half_c = 0.99 * opacity, -0.5 * conic_a, -0.5 * conic_c
    across = iota((SIDE, depth), 0).astype(F32) - 7.5

    def chunk(t, i):
        return pl.ds(pl.multiple_of(t * pix + i * SIDE, SIDE), SIDE)

    def of(t):
        return slice(t * depth, (t + 1) * depth)

    def over_rows(body, init, t):
        return lax.fori_loop(0, pix // SIDE, functools.partial(body, t), init, unroll=UNROLL)

    def save(rows, x):
        for n, piece in enumerate(parts(x, 2)):
            split_s[n, rows] = piece

    for t in range(tiles):
        delta_u = across - screen_u[:, of(t)]
        first = half_a[:, of(t)] * delta_u * delta_u
        mixed = -conic_b[:, of(t)] * delta_u

        def forward(t, i, carry, first=first, mixed=mixed):
            rows = chunk(t, i)
            delta_v = (i.astype(F32) - 7.5) - screen_v[:, of(t)]
            power = first + delta_v * (mixed + half_c[:, of(t)] * delta_v)
            alpha = peak[:, of(t)] * jnp.exp(power)
            alpha_s[rows] = alpha
            save(rows, jnp.log(1.0 - alpha))
            return carry

        over_rows(forward, 0, t)
    half = depth // 2
    tri = one_hot(iota((half, half), 0) < iota((half, half), 1))
    full = jnp.ones((half, half), BF16)
    run_s[:, :half] = dot(split_s[0, :, :half], tri) + dot(split_s[1, :, :half], tri)
    run_s[:, half:] = (
        dot(split_s[0, :, half:], tri) + dot(split_s[1, :, half:], tri)
        + dot(split_s[0, :, :half], full) + dot(split_s[1, :, :half], full)
    )
    ones = jnp.ones((16, depth), BF16)
    behind = dot_t(ones, split_s[0]) + dot_t(ones, split_s[1])
    behind = BACKGROUND * jnp.exp(behind[0:1])
    for t in range(tiles):

        def weigh(t, i, carry):
            rows = chunk(t, i)
            through = jnp.exp(run_s[rows])
            run_s[rows] = through
            save(rows, alpha_s[rows] * through)
            return carry

        over_rows(weigh, 0, t)
    color_grads, tails = [], []
    for t in range(tiles):
        px = slice(t * pix, (t + 1) * pix)
        paints = parts(colors[:, of(t)])
        paint = stacked(paints)
        shown = groups(dot_t(paint, split_s[0, px]) + dot_t(paint, split_s[1, px]))
        shown = shown + behind[:, px]
        gaps = []
        for c in range(3):
            image_ref[c, t : t + 1] = shown[c : c + 1]
            gaps.append(shown[c : c + 1] - target_ref[c, t : t + 1])
        tail = behind[:, px] * (gaps[0] + gaps[1] + gaps[2])
        gap = jnp.concatenate([*gaps, jnp.zeros((5, pix), F32)], axis=0)
        gap_parts = parts(gap)
        drawn = stacked(gap_parts)
        color_grads.append(groups(dot(drawn, split_s[0, px]) + dot(drawn, split_s[1, px])))
        high, middle, low = [piece.astype(F32) for piece in gap_parts]
        ends = [piece.astype(F32) for piece in parts(tail)]
        ends = jnp.concatenate([*ends, jnp.zeros((5, pix), F32)], axis=0)
        left = jnp.concatenate(
            [high, high, high, middle, middle, low, ends, jnp.zeros((72, pix), F32)], axis=0
        )
        left = jnp.concatenate(
            [jnp.transpose(left[:, :128]), jnp.transpose(left[:, 128:])], axis=0
        ).astype(BF16)
        high, middle, low = [piece.astype(F32) for piece in paints]
        right = jnp.concatenate(
            [high, middle, low, high, middle, high, jnp.zeros((80, depth), F32)], axis=0
        ).astype(BF16)
        slope_s[px] = dot(left, right)
        row = iota((128, depth), 0)
        tails.append(dot(left, one_hot((row >= 48) & (row < 51))))
    for t in range(tiles):

        def spread_back(t, i, carry):
            rows = chunk(t, i)
            through_slope = run_s[rows] * slope_s[rows]
            slope_s[rows] = through_slope
            save(rows, alpha_s[rows] * through_slope)
            return carry

        over_rows(spread_back, 0, t)
    tri = one_hot(iota((half, half), 0) > iota((half, half), 1))
    for t in range(tiles):
        px = slice(t * pix, (t + 1) * pix)
        run_s[px, half:] = (
            dot(split_s[0, px, half:], tri) + dot(split_s[1, px, half:], tri)
            + tails[t][:, half:]
        )
        run_s[px, :half] = (
            dot(split_s[0, px, :half], tri) + dot(split_s[1, px, :half], tri)
            + dot(split_s[0, px, half:], full) + dot(split_s[1, px, half:], full)
            + tails[t][:, :half]
        )
    sums = []
    for t in range(tiles):

        def backward(t, i, sums):
            rows = chunk(t, i)
            alpha = alpha_s[rows]
            pull = alpha * (slope_s[rows] - run_s[rows] / (1.0 - alpha))
            delta_v = (i.astype(F32) - 7.5) - screen_v[:, of(t)]
            pull_v = pull * delta_v
            return sums[0] + pull, sums[1] + pull_v, sums[2] + pull_v * delta_v

        zero = jnp.zeros((SIDE, depth), F32)
        plain, with_v, with_vv = over_rows(backward, (zero, zero, zero), t)
        delta_u = across - screen_u[:, of(t)]
        plain_u = plain * delta_u
        sums.append(
            [
                jnp.sum(a, axis=0, keepdims=True)
                for a in (plain, plain_u, with_v, plain_u * delta_u, with_v * delta_u, with_vv)
            ]
        )
    s_0, s_u, s_v, s_uu, s_uv, s_vv = [
        jnp.concatenate([s[n] for s in sums], axis=1) for n in range(6)
    ]
    entry_s[0:1] = conic_a * s_u + conic_b * s_v
    entry_s[1:2] = conic_b * s_u + conic_c * s_v
    entry_s[2:3] = -0.5 * s_uu
    entry_s[3:4] = -s_uv
    entry_s[4:5] = -0.5 * s_vv
    entry_s[5:6] = s_0 / opacity
    entry_s[6:9] = jnp.concatenate(color_grads, axis=1)[0:3]
    entry_s[9:10] = (owner * SUB + ids % SUB).astype(F32)
    grads = entry_s[...]
    entry_ref[...] = grads
    home = (values[9] + 0.5).astype(jnp.int32)
    order, moves = rank_of(home, devices)
    slots = iota((32, entries), 0) == jnp.where(order < HOME_CAP, order, 99)
    sent = 0.0
    for piece in parts(grads, 2):
        piece = piece.astype(F32)
        rows = jnp.concatenate(
            [jnp.where(slots, piece[r : r + 1], 0.0).astype(BF16) for r in range(SENT)], axis=0
        )
        sent = sent + dot_t(rows, moves)
    for r in range(SENT):
        sent_s[r * HOME_CAP : (r + 1) * HOME_CAP] = sent[r * 32 : r * 32 + HOME_CAP]
    over = jnp.max(order, axis=1, keepdims=True) >= HOME_CAP
    flag = jnp.where(over, 1.0, 0.0) + jnp.zeros((256 - SENT * HOME_CAP, devices), F32)
    sent_s[SENT * HOME_CAP :] = flag
    grad_ref[:, :128] = jnp.transpose(sent_s[:128])
    grad_ref[:, 128:] = jnp.transpose(sent_s[128:])


def pull_back(total, old, camera_ref, out_ref):
    cam = [camera_ref[0, i] for i in range(8)]
    g_u, g_v, g_a, g_b, g_c = [total[r : r + 1] for r in range(5)]
    conic_a, conic_c, skew, root = conics(old)
    half_b = g_b * (0.45 * skew * root)
    level = sigmoid(old[6:10])
    rows = [
        (0, cam[0] * g_u + cam[4] * g_v),
        (1, cam[1] * g_u + cam[5] * g_v),
        (2, cam[2] * g_u + cam[6] * g_v),
        (3, g_a * conic_a + half_b),
        (4, g_b * 0.9 * (1.0 - skew * skew) * root),
        (5, g_c * conic_c + half_b),
        (6, total[5:9] * level * (1.0 - level)),
    ]
    for copy in range(out_ref.shape[0]):
        for r, value in rows:
            out_ref[copy, r : r + value.shape[0]] = value


def collect_body(grad_ref, request_ref, response_ref, camera_ref, out_ref, old_ref, came_s):
    settle(request_ref, response_ref, old_ref)
    gauss = out_ref.shape[2]
    devices = grad_ref.shape[0]
    came_s[:128] = jnp.transpose(grad_ref[:, :128])
    came_s[128:] = jnp.transpose(grad_ref[:, 128:])
    spots = (came_s[9 * HOME_CAP : 10 * HOME_CAP] + 0.5).astype(jnp.int32)
    hot, came = [], []
    zero = jnp.zeros((6, devices), F32)
    for j in range(HOME_CAP):
        hot.append(one_hot(iota((gauss, devices), 0) == spots[j : j + 1]))
        came.append(jnp.concatenate([came_s[pl.ds(j, SENT, stride=HOME_CAP), :], zero], axis=0))
    came = parts(jnp.concatenate(came, axis=1), 2)
    total = dot_t(jnp.concatenate(came, axis=0), jnp.concatenate(hot, axis=1))
    out_ref[...] = jnp.zeros_like(out_ref)
    pull_back(total[:ROWS] + total[ROWS:], old_ref[...], camera_ref, out_ref)
    flags = came_s[SENT * HOME_CAP :]
    flag = jnp.max(jnp.max(flags, axis=1, keepdims=True), axis=0, keepdims=True)
    for copy in range(out_ref.shape[0]):
        out_ref[copy, 10:11] = flag + jnp.zeros((1, gauss), F32)


def to_owner_body(entry_ref, lists_ref, out_ref):
    devices = out_ref.shape[0]
    rank = lists_ref[2:3]
    named = one_hot(iota((devices, rank.shape[1]), 0) == lists_ref[0:1])
    grads = entry_ref[...]
    slots = jnp.concatenate([jnp.where(rank == j, grads, 0.0) for j in range(CAP)], axis=0)
    sent = sum(dot_t(piece, named) for piece in parts(slots))
    out_ref[:, :128] = jnp.transpose(sent[:128])
    out_ref[:, 128:] = jnp.transpose(sent[128:])


def at_owner_body(grad_ref, request_ref, lists_ref, out_ref, *, gauss):
    devices = grad_ref.shape[0]
    came = jnp.concatenate(
        [jnp.transpose(grad_ref[:, :128]), jnp.transpose(grad_ref[:, 128:])], axis=0
    )
    came = jnp.concatenate([came[j * ROWS : (j + 1) * ROWS] for j in range(CAP)], axis=1)
    total = dot_t(jnp.concatenate(parts(came), axis=0), asked_hot(request_ref, gauss))
    total = total[:ROWS] + total[ROWS : 2 * ROWS] + total[2 * ROWS :]
    stack = jnp.concatenate([total, jnp.zeros_like(total)], axis=0)
    out_ref[...] = pack_blocks(stack, lists_ref[3:4, 0:gauss].astype(F32), devices, 32)


def at_home_body(came_ref, old_ref, camera_ref, out_ref):
    out_ref[...] = jnp.zeros_like(out_ref)
    devices = came_ref.shape[0]
    came = jnp.transpose(came_ref[...])
    sub = old_ref.shape[1] // devices
    total = place_blocks([came[i * 32 : (i + 1) * 32] for i in range(sub)], devices)
    pull_back(total, old_ref[...], camera_ref, out_ref)


def adam_body(grads_ref, old_ref, params_ref, moment1_ref, moment2_ref, full_ref):
    old = old_ref[...]
    grad = (grads_ref[0] + grads_ref[1]) + (grads_ref[2] + grads_ref[3])
    full_ref[0, 0] = (jnp.max(grad[10:11]) > 0.5).astype(jnp.int32)
    grad = grad[0:10]
    moment1 = 0.9 * old[10:20] + 0.1 * grad
    moment2 = 0.99 * old[20:30] + 0.01 * grad * grad
    params_ref[...] = old[0:10] - 0.01 * moment1 / (jnp.sqrt(moment2) + 1e-08)
    moment1_ref[...] = moment1
    moment2_ref[...] = moment2


def shape(*dims, dtype=F32):
    return jax.ShapeDtypeStruct(dims, dtype)


def exchange(x):
    devices = lax.axis_size("dev")
    parcel = x.reshape(devices, -1, 128)
    return lax.all_to_all(parcel, "dev", 0, 0, tiled=True).reshape(x.shape)


def share(copies):
    return lax.all_to_all(copies, "rep", 0, 0, tiled=True)


def local(params, moment1, moment2, camera, owner, local_index, target, rehome):
    devices = lax.axis_size("dev")
    reps = lax.axis_size("rep")
    gauss = params.shape[1]
    _, tiles, depth = local_index.shape
    entries = tiles * depth
    pix = target.shape[3]
    owners = owner.reshape(1, entries)
    ids = local_index[0]
    stack = pltpu.VMEM((32, gauss), F32)
    request, lists = call(
        request_body,
        (shape(devices, 128), shape(8, entries, dtype=jnp.int32)),
        [
            pltpu.VMEM((1, entries), jnp.int32), pltpu.VMEM((tiles, depth), jnp.int32),
            pltpu.VMEM((10, gauss), F32), pltpu.VMEM((1, devices), jnp.int32), stack,
            pltpu.VMEM((devices, 128), F32), pltpu.VMEM((8, entries), jnp.int32),
            pltpu.SemaphoreType.DMA((6,)),
        ],
        hbm=(0, 1, 2, 3),
        hbm_out=(0, 1),
        vmem=60 * 1024 * 1024,
    )(owners, ids, moment2, rehome)
    request = exchange(request)
    table, blocks, lists, goal = call(
        table_body,
        (
            shape(ROWS, gauss), shape(256 - VALUES * CAP, devices),
            shape(8, entries, dtype=jnp.int32), shape(3, tiles, pix),
        ),
        [stack],
        smem=(2,),
    )(params, moment1, camera, lists, target[0].transpose(1, 0, 2))
    response = call(respond_body, shape(devices, 256), [pltpu.VMEM((256, devices), F32)])(
        request, table, blocks
    )
    response = exchange(response)
    plane = pltpu.VMEM((tiles * pix, depth), F32)
    images, grads, by_entry = call(
        composite_body,
        (shape(3, tiles, pix), shape(devices, 256), shape(ROWS, entries)),
        [
            plane, plane, plane, pltpu.VMEM((2, tiles * pix, depth), BF16),
            pltpu.VMEM((ROWS, entries), F32), pltpu.VMEM((256, devices), F32),
        ],
    )(response, lists, goal)
    grads = exchange(grads)
    grads, old = call(
        collect_body,
        (shape(reps, ROWS, gauss), shape(32, gauss)),
        [pltpu.VMEM((256, devices), F32)],
        smem=(3,),
    )(grads, request, response, camera)
    update = call(
        adam_body, (shape(10, gauss),) * 3 + (shape(1, 1, dtype=jnp.int32),), smem_out=(3,)
    )
    *out, full = update(share(grads), old)

    def by_owner(out, by_entry, lists, request, old, camera):
        sent = call(to_owner_body, shape(devices, 256))(by_entry, lists)
        sent = call(functools.partial(at_owner_body, gauss=gauss), shape(devices, 128))(
            exchange(sent), request, lists
        )
        sent = call(at_home_body, shape(reps, ROWS, gauss), smem=(2,))(
            exchange(sent), old, camera
        )
        return list(update(share(sent), old)[:3])

    out = lax.cond(
        full[0, 0] > 0, by_owner, lambda out, *rest: out,
        list(out), by_entry, lists, request, old, camera,
    )
    return (*out, images.transpose(1, 0, 2)[None])


def solution(mesh):
    in_specs = (
        P(None, "dev"),
        P(None, "dev"),
        P(None, "dev"),
        P("rep", None),
        P("rep", "dev", None, None),
        P("rep", "dev", None),
        P("rep", "dev", None, None),
        P("dev", None),
    )
    out_specs = (P(None, "dev"), P(None, "dev"), P(None, "dev"), P("rep", "dev", None, None))
    return jax.shard_map(local, mesh=mesh, in_specs=in_specs, out_specs=out_specs, check_vma=False)
```

```python
import functools

import jax
import jax.numpy as jnp
from jax import lax
from jax.experimental import pallas as pl
from jax.experimental.pallas import tpu as pltpu
from jax.sharding import PartitionSpec as P

SIDE = 16
BACKGROUND = 0.5
CAP = 16
SUB = 4
HOME_CAP = 25
SENT = 10
VALUES = 10
UNROLL = 16
ROWS = 16
VMEM = 40 * 1024 * 1024
F32 = jnp.float32
BF16 = jnp.bfloat16


def one_hot(condition):
    return jnp.where(condition, 1.0, 0.0).astype(BF16)


def parts(x, count=3):
    out = []
    for _ in range(count):
        piece = x.astype(BF16)
        out.append(piece)
        x = x - piece.astype(F32)
    return out


def iota(shape, dim):
    return lax.broadcasted_iota(jnp.int32, shape, dim)


def dot(a, b):
    return lax.dot_general(a, b, (((1,), (0,)), ((), ())), preferred_element_type=F32)


def dot_t(a, b):
    return lax.dot_general(a, b, (((1,), (1,)), ((), ())), preferred_element_type=F32)


def call(body, out_shape, scratch=(), smem=(), hbm=(), smem_out=(), hbm_out=(), vmem=VMEM):
    def run(*args):
        space = [
            pltpu.SMEM if i in smem else pl.ANY if i in hbm else pltpu.VMEM
            for i in range(len(args))
        ]
        outs = jax.tree.map(lambda _: pl.BlockSpec(memory_space=pltpu.VMEM), out_shape)
        if smem_out or hbm_out:
            outs = tuple(
                pl.BlockSpec(
                    memory_space=pltpu.SMEM if i in smem_out else pl.ANY if i in hbm_out else pltpu.VMEM
                )
                for i in range(len(out_shape))
            )
        return pl.pallas_call(
            body,
            out_shape=out_shape,
            in_specs=[pl.BlockSpec(memory_space=m) for m in space],
            out_specs=outs,
            scratch_shapes=list(scratch),
            compiler_params=pltpu.CompilerParams(vmem_limit_bytes=vmem),
        )(*args)

    return run


def start(source, place, sem):
    copy = pltpu.make_async_copy(source, place, sem)
    copy.start()
    return copy


def along(ref):
    return jnp.concatenate([ref[t : t + 1] for t in range(ref.shape[0])], axis=1)


def rank_of(device, devices):
    entries = device.shape[1]
    step = 256
    before = one_hot(iota((step, step), 0) < iota((step, step), 1))
    steps = [device[:, start : start + step] for start in range(0, entries, step)]
    named = [jnp.where(iota((devices, step), 0) == d, 1.0, 0.0) for d in steps]
    count = dot(jnp.concatenate(named, axis=0).astype(BF16), before)
    base = jnp.zeros((devices, 1), F32)
    ranks = []
    for n, hot in enumerate(named):
        place = count[n * devices : (n + 1) * devices] + base
        base = base + jnp.sum(hot, axis=1, keepdims=True)
        ranks.append(jnp.sum(hot * place, axis=0, keepdims=True).astype(jnp.int32))
    return jnp.concatenate(ranks, axis=1), jnp.concatenate(named, axis=1).astype(BF16)


def homes_of(rehome_ref, gauss):
    devices = rehome_ref.shape[1]
    sub = gauss // devices
    homes = jnp.broadcast_to(rehome_ref[...].astype(F32), (8, devices)).astype(BF16)
    return dot(homes, one_hot(iota((devices, gauss), 1) // sub == iota((devices, gauss), 0)))[0:1]


def pack_blocks(stack, homes, devices, rows):
    gauss = stack.shape[1]
    sub = gauss // devices
    place = iota((devices, gauss), 0) == homes.astype(jnp.int32)
    within = iota((devices, gauss), 1) % sub
    pick = jnp.concatenate([one_hot(place & (within == i)) for i in range(sub)], axis=0)
    moved = dot_t(jnp.concatenate(parts(stack), axis=0), pick)
    moved = moved[:32] + moved[32:64] + moved[64:]
    moved = [moved[:rows, i * devices : (i + 1) * devices] for i in range(sub)]
    if sub * rows < 128:
        moved.append(jnp.zeros((128 - sub * rows, devices), F32))
    return jnp.transpose(jnp.concatenate(moved, axis=0))[:, : sub * rows]


def in_order(gauss, devices):
    sub = gauss // devices
    row = iota((gauss, gauss), 0)
    return one_hot(row % devices * sub + row // devices == iota((gauss, gauss), 1))


def sigmoid(x):
    return 1.0 / (1.0 + jnp.exp(-x))


def conics(rows):
    conic_a, conic_c, skew = jnp.exp(rows[3:4]), jnp.exp(rows[5:6]), jnp.tanh(rows[4:5])
    return conic_a, conic_c, skew, jnp.sqrt(conic_a * conic_c)


def request_body(
    owner_hbm, index_hbm, moment2_hbm, rehome_hbm,
    request_hbm, lists_hbm,
    owner_s, index_s, moment2_s, rehome_s, stack_s, request_s, lists_s, sems,
):
    copies = [
        start(source, place, sems.at[n])
        for n, (source, place) in enumerate(
            [
                (owner_hbm, owner_s), (index_hbm, index_s),
                (rehome_hbm, rehome_s), (moment2_hbm, moment2_s),
            ]
        )
    ]
    gauss = moment2_s.shape[1]
    devices = request_s.shape[0]
    stack_s[...] = jnp.zeros_like(stack_s)
    lists_s[...] = jnp.zeros_like(lists_s)
    for copy in copies:
        copy.wait()
    owner, ids = owner_s[...], along(index_s)
    rank, named = rank_of(owner, devices)
    homes = homes_of(rehome_s, gauss)
    lists_s[3:4, 0:gauss] = homes.astype(jnp.int32)
    lists_s[0:1] = owner
    lists_s[1:2] = ids
    lists_s[2:3] = rank
    kept = start(lists_s, lists_hbm, sems.at[4])
    slot = iota((CAP, ids.shape[1]), 0) == rank
    high = jnp.where(slot, (ids >> 4).astype(F32), 0.0)
    low = jnp.where(slot, (ids & 15).astype(F32), 0.0)
    total = dot_t(named, jnp.concatenate([high, low], axis=0).astype(BF16))
    asked = 16.0 * total[:, :CAP] + total[:, CAP:]
    stack_s[0:10] = moment2_s[...]
    blocks = pack_blocks(stack_s[...], homes, devices, 16)
    zero = jnp.zeros((devices, 128 - CAP - blocks.shape[1]), F32)
    request_s[...] = jnp.concatenate([blocks, asked, zero], axis=1)
    sent = start(request_s, request_hbm, sems.at[5])
    kept.wait()
    sent.wait()


def table_body(
    params_ref, moment1_ref, camera_ref, lists_ref, target_ref,
    table_ref, blocks_ref, kept_lists_ref, kept_target_ref, order_ref, stack_s,
):
    kept_lists_ref[...] = lists_ref[...]
    kept_target_ref[...] = target_ref[...]
    gauss = params_ref.shape[1]
    devices = blocks_ref.shape[1]
    cam = [camera_ref[0, i] for i in range(8)]
    homes = lists_ref[3:4, 0:gauss].astype(F32)
    order_ref[...] = in_order(gauss, devices)
    params = params_ref[...]
    stack_s[...] = jnp.zeros_like(stack_s)
    stack_s[0:10] = params
    stack_s[10:20] = moment1_ref[...]
    blocks = pack_blocks(stack_s[...], homes, devices, 24)
    zero = jnp.zeros((devices, 128 - blocks.shape[1]), F32)
    blocks = jnp.transpose(jnp.concatenate([blocks, zero], axis=1))
    blocks_ref[...] = blocks[: blocks_ref.shape[0]]
    x, y, z = params[0:1], params[1:2], params[2:3]
    conic_a, conic_c, skew, root = conics(params)
    table_ref[...] = jnp.zeros_like(table_ref)
    table_ref[0:1] = cam[0] * x + cam[1] * y + cam[2] * z + cam[3]
    table_ref[1:2] = cam[4] * x + cam[5] * y + cam[6] * z + cam[7]
    table_ref[2:3] = conic_a
    table_ref[3:4] = 0.9 * skew * root
    table_ref[4:5] = conic_c
    table_ref[5:9] = sigmoid(params[6:10])
    table_ref[9:10] = homes


def asked_hot(request_ref, gauss):
    devices = request_ref.shape[0]
    ids = jnp.transpose(request_ref[...])[64 : 64 + CAP].astype(jnp.int32)
    return jnp.concatenate(
        [one_hot(iota((gauss, devices), 0) == ids[j : j + 1]) for j in range(CAP)], axis=1
    )


def respond_body(request_ref, table_ref, blocks_ref, response_ref, out_s):
    devices = request_ref.shape[0]
    sub = table_ref.shape[1] // devices
    ids = jnp.transpose(request_ref[...])[64 : 64 + CAP].astype(jnp.int32)
    ids = jnp.concatenate([ids[j : j + 1] for j in range(CAP)], axis=1)
    hot = one_hot(iota((devices, ids.shape[1]), 0) == ids % devices)
    pieces = parts(table_ref[...])
    tables = [
        piece[:, i * devices : (i + 1) * devices] for piece in pieces for i in range(sub)
    ]
    all_got = dot(jnp.concatenate(tables, axis=0), hot)
    span = sub * ROWS
    all_got = all_got[:span] + all_got[span : 2 * span] + all_got[2 * span :]
    got = jnp.zeros((ROWS, ids.shape[1]), F32)
    for i in range(sub):
        got = got + jnp.where(ids // devices == i, all_got[i * ROWS : (i + 1) * ROWS], 0.0)
    for j in range(CAP):
        out_s[pl.ds(j, VALUES, stride=CAP), :] = got[:VALUES, j * devices : (j + 1) * devices]
    out_s[VALUES * CAP :] = blocks_ref[...]
    response_ref[:, :128] = jnp.transpose(out_s[:128])
    response_ref[:, 128:] = jnp.transpose(out_s[128:])


def settle(request_ref, response_ref, old_ref):
    devices = request_ref.shape[0]
    sub = old_ref.shape[1] // devices
    first = jnp.transpose(request_ref[...])
    second = jnp.transpose(response_ref[:, 128:])[VALUES * CAP - 128 :]
    for i in range(sub):
        cols = slice(i * devices, (i + 1) * devices)
        old_ref[0:24, cols] = second[i * 24 : i * 24 + 24]
        old_ref[24:40, cols] = first[i * 16 : i * 16 + 16]


def stacked(pieces):
    rows = [piece.astype(F32) for piece in pieces]
    return jnp.concatenate([*rows, jnp.zeros_like(rows[0])], axis=0).astype(BF16)


def groups(x):
    return x[0:8] + x[8:16] + x[16:24]


def composite_body(
    response_ref, lists_ref, target_ref,
    image_ref, grad_ref, entry_ref,
    alpha_s, run_s, slope_s, split_s, entry_s,
):
    devices = response_ref.shape[0]
    entries = lists_ref.shape[1]
    _, tiles, pix = target_ref.shape
    depth = entries // tiles
    owner, ids, rank = lists_ref[0:1], lists_ref[1:2], lists_ref[2:3]
    named = one_hot(iota((devices, entries), 0) == owner)
    got = jnp.concatenate(
        [jnp.transpose(response_ref[:, :128]), jnp.transpose(response_ref[:, 128:])], axis=0
    )[: VALUES * CAP]
    spread = dot(jnp.concatenate(parts(got), axis=0), named)
    span = VALUES * CAP
    spread = spread[:span] + spread[span : 2 * span] + spread[2 * span :]
    mine = iota((CAP, entries), 0) == rank
    values = [
        jnp.sum(jnp.where(mine, spread[r * CAP : (r + 1) * CAP], 0.0), axis=0, keepdims=True)
        for r in range(VALUES)
    ]
    screen_u, screen_v, conic_a, conic_b, conic_c, opacity = values[:6]
    entry_s[...] = jnp.zeros_like(entry_s)
    for c in range(3):
        entry_s[c : c + 1] = values[6 + c] - BACKGROUND
    colors = entry_s[0:8]
    peak, half_a, half_c = 0.99 * opacity, -0.5 * conic_a, -0.5 * conic_c
    across = iota((SIDE, depth), 0).astype(F32) - 7.5

    def chunk(t, i):
        return pl.ds(pl.multiple_of(t * pix + i * SIDE, SIDE), SIDE)

    def of(t):
        return slice(t * depth, (t + 1) * depth)

    def over_rows(body, init, t):
        return lax.fori_loop(0, pix // SIDE, functools.partial(body, t), init, unroll=UNROLL)

    def save(rows, x):
        for n, piece in enumerate(parts(x, 2)):
            split_s[n, rows] = piece

    for t in range(tiles):
        delta_u = across - screen_u[:, of(t)]
        first = half_a[:, of(t)] * delta_u * delta_u
        mixed = -conic_b[:, of(t)] * delta_u

        def forward(t, i, carry, first=first, mixed=mixed):
            rows = chunk(t, i)
            delta_v = (i.astype(F32) - 7.5) - screen_v[:, of(t)]
            power = first + delta_v * (mixed + half_c[:, of(t)] * delta_v)
            alpha = peak[:, of(t)] * jnp.exp(power)
            alpha_s[rows] = alpha
            save(rows, jnp.log(1.0 - alpha))
            return carry

        over_rows(forward, 0, t)
    half = depth // 2
    tri = one_hot(iota((half, half), 0) < iota((half, half), 1))
    full = jnp.ones((half, half), BF16)
    run_s[:, :half] = dot(split_s[0, :, :half], tri) + dot(split_s[1, :, :half], tri)
    run_s[:, half:] = (
        dot(split_s[0, :, half:], tri) + dot(split_s[1, :, half:], tri)
        + dot(split_s[0, :, :half], full) + dot(split_s[1, :, :half], full)
    )
    for t in range(tiles):

        def weigh(t, i, carry):
            rows = chunk(t, i)
            through = jnp.exp(run_s[rows])
            run_s[rows] = through
            save(rows, alpha_s[rows] * through)
            return carry

        over_rows(weigh, 0, t)
    color_grads = []
    for t in range(tiles):
        px = slice(t * pix, (t + 1) * pix)
        paints = parts(colors[:, of(t)])
        paint = stacked(paints)
        shown = groups(dot_t(paint, split_s[0, px]) + dot_t(paint, split_s[1, px]))
        shown = shown + BACKGROUND
        gaps = []
        for c in range(3):
            image_ref[c, t : t + 1] = shown[c : c + 1]
            gaps.append(shown[c : c + 1] - target_ref[c, t : t + 1])
        gap = jnp.concatenate([*gaps, jnp.zeros((5, pix), F32)], axis=0)
        gap_parts = parts(gap)
        drawn = stacked(gap_parts)
        color_grads.append(groups(dot(drawn, split_s[0, px]) + dot(drawn, split_s[1, px])))
        high, middle, low = [piece.astype(F32) for piece in gap_parts]
        left = jnp.concatenate(
            [high, high, high, middle, middle, low, jnp.zeros((80, pix), F32)], axis=0
        )
        left = jnp.concatenate(
            [jnp.transpose(left[:, :128]), jnp.transpose(left[:, 128:])], axis=0
        ).astype(BF16)
        high, middle, low = [piece.astype(F32) for piece in paints]
        right = jnp.concatenate(
            [high, middle, low, high, middle, high, jnp.zeros((80, depth), F32)], axis=0
        ).astype(BF16)
        slope_s[px] = dot(left, right)
    for t in range(tiles):

        def spread_back(t, i, carry):
            rows = chunk(t, i)
            through_slope = run_s[rows] * slope_s[rows]
            slope_s[rows] = through_slope
            save(rows, alpha_s[rows] * through_slope)
            return carry

        over_rows(spread_back, 0, t)
    tri = one_hot(iota((half, half), 0) > iota((half, half), 1))
    run_s[:, half:] = dot(split_s[0, :, half:], tri) + dot(split_s[1, :, half:], tri)
    run_s[:, :half] = (
        dot(split_s[0, :, :half], tri) + dot(split_s[1, :, :half], tri)
        + dot(split_s[0, :, half:], full) + dot(split_s[1, :, half:], full)
    )
    sums = []
    for t in range(tiles):

        def backward(t, i, sums):
            rows = chunk(t, i)
            alpha = alpha_s[rows]
            pull = alpha * (slope_s[rows] - run_s[rows] / (1.0 - alpha))
            delta_v = (i.astype(F32) - 7.5) - screen_v[:, of(t)]
            pull_v = pull * delta_v
            return sums[0] + pull, sums[1] + pull_v, sums[2] + pull_v * delta_v

        zero = jnp.zeros((SIDE, depth), F32)
        plain, with_v, with_vv = over_rows(backward, (zero, zero, zero), t)
        delta_u = across - screen_u[:, of(t)]
        plain_u = plain * delta_u
        sums.append(
            [
                jnp.sum(a, axis=0, keepdims=True)
                for a in (plain, plain_u, with_v, plain_u * delta_u, with_v * delta_u, with_vv)
            ]
        )
    s_0, s_u, s_v, s_uu, s_uv, s_vv = [
        jnp.concatenate([s[n] for s in sums], axis=1) for n in range(6)
    ]
    entry_s[0:1] = conic_a * s_u + conic_b * s_v
    entry_s[1:2] = conic_b * s_u + conic_c * s_v
    entry_s[2:3] = -0.5 * s_uu
    entry_s[3:4] = -s_uv
    entry_s[4:5] = -0.5 * s_vv
    entry_s[5:6] = s_0 / opacity
    entry_s[6:9] = jnp.concatenate(color_grads, axis=1)[0:3]
    entry_s[9:10] = (owner * SUB + ids % SUB).astype(F32)
    grads = entry_s[...]
    entry_ref[...] = grads
    home = (values[9] + 0.5).astype(jnp.int32)
    order, moves = rank_of(home, devices)
    lanes = grad_ref.shape[1]
    row = iota((8, entries), 0)
    pieces = [piece.astype(F32) for piece in parts(grads, 2)]
    sent = [[], []]
    for start_row in range(0, lanes, 8):
        c, last = start_row // HOME_CAP, (start_row + 7) // HOME_CAP
        here = row == order - (start_row - c * HOME_CAP)
        if last > c:
            first = row < last * HOME_CAP - start_row
            here = (here & first) | (row == order - (start_row - last * HOME_CAP))
        for n in range(2):
            value = pieces[n][c : c + 1]
            if last > c:
                value = jnp.where(first, value, pieces[n][last : last + 1])
            sent[n].append(jnp.where(here, value, 0.0))
    sent = [jnp.concatenate(rows, axis=0).astype(BF16) for rows in sent]
    sent = dot_t(jnp.concatenate(sent, axis=0), moves)
    sent = sent[:lanes] + sent[lanes:]
    sent = jnp.concatenate([jnp.transpose(sent[:128]), jnp.transpose(sent[128:])], axis=1)
    over = jnp.max(order, axis=1, keepdims=True) >= HOME_CAP
    flag = jnp.where(over, 1.0, 0.0)
    grad_ref[...] = jnp.where(iota((devices, lanes), 1) < SENT * HOME_CAP, sent, flag)


def pull_back(total, old, camera_ref, out_ref):
    cam = [camera_ref[0, i] for i in range(8)]
    g_u, g_v, g_a, g_b, g_c = [total[r : r + 1] for r in range(5)]
    conic_a, conic_c, skew, root = conics(old)
    half_b = g_b * (0.45 * skew * root)
    level = sigmoid(old[6:10])
    out_ref[0:1] = cam[0] * g_u + cam[4] * g_v
    out_ref[1:2] = cam[1] * g_u + cam[5] * g_v
    out_ref[2:3] = cam[2] * g_u + cam[6] * g_v
    out_ref[3:4] = g_a * conic_a + half_b
    out_ref[4:5] = g_b * 0.9 * (1.0 - skew * skew) * root
    out_ref[5:6] = g_c * conic_c + half_b
    out_ref[6:10] = total[5:9] * level * (1.0 - level)


def collect_body(
    grad_ref, request_ref, response_ref, camera_ref, out_hbm, old_ref, came_s, total_s, sems
):
    settle(request_ref, response_ref, old_ref)
    devices = grad_ref.shape[0]
    sub = old_ref.shape[1] // devices
    came_s[:128] = jnp.transpose(grad_ref[:, :128])
    came_s[128:] = jnp.transpose(grad_ref[:, 128:])
    spots = (came_s[9 * HOME_CAP : 10 * HOME_CAP] + 0.5).astype(jnp.int32)
    blocks, places = spots // sub, spots % sub
    hot, came = [], []
    zero = jnp.zeros((6, devices), F32)
    for j in range(HOME_CAP):
        hot.append(one_hot(iota((devices, devices), 0) == blocks[j : j + 1]))
        slot = jnp.concatenate([came_s[pl.ds(j, SENT, stride=HOME_CAP), :], zero], axis=0)
        place = places[j : j + 1]
        came.append(
            jnp.concatenate([jnp.where(place == i, slot, 0.0) for i in range(sub)], axis=0)
        )
    came = parts(jnp.concatenate(came, axis=1), 2)
    total = dot_t(jnp.concatenate(came, axis=0), jnp.concatenate(hot, axis=1))
    total = total[: sub * ROWS] + total[sub * ROWS :]
    total = jnp.concatenate([total[i * ROWS : (i + 1) * ROWS] for i in range(sub)], axis=1)
    total_s[...] = jnp.zeros_like(total_s)
    pull_back(total, old_ref[...], camera_ref, total_s)
    flags = came_s[SENT * HOME_CAP :]
    flag = jnp.max(jnp.max(flags, axis=1, keepdims=True), axis=0, keepdims=True)
    total_s[10:11] = flag + jnp.zeros((1, total_s.shape[1]), F32)
    copies = [start(total_s, out_hbm.at[n], sems.at[n]) for n in range(out_hbm.shape[0])]
    for copy in copies:
        copy.wait()


def to_owner_body(entry_ref, lists_ref, out_ref):
    devices = out_ref.shape[0]
    rank = lists_ref[2:3]
    named = one_hot(iota((devices, rank.shape[1]), 0) == lists_ref[0:1])
    grads = entry_ref[...]
    slots = jnp.concatenate([jnp.where(rank == j, grads, 0.0) for j in range(CAP)], axis=0)
    sent = sum(dot_t(piece, named) for piece in parts(slots))
    out_ref[:, :128] = jnp.transpose(sent[:128])
    out_ref[:, 128:] = jnp.transpose(sent[128:])


def at_owner_body(grad_ref, request_ref, lists_ref, out_ref, *, gauss):
    devices = grad_ref.shape[0]
    came = jnp.concatenate(
        [jnp.transpose(grad_ref[:, :128]), jnp.transpose(grad_ref[:, 128:])], axis=0
    )
    came = jnp.concatenate([came[j * ROWS : (j + 1) * ROWS] for j in range(CAP)], axis=1)
    total = dot_t(jnp.concatenate(parts(came), axis=0), asked_hot(request_ref, gauss))
    total = total[:ROWS] + total[ROWS : 2 * ROWS] + total[2 * ROWS :]
    stack = jnp.concatenate([total, jnp.zeros_like(total)], axis=0)
    out_ref[...] = pack_blocks(stack, lists_ref[3:4, 0:gauss].astype(F32), devices, 32)


def at_home_body(came_ref, old_ref, camera_ref, out_ref, total_s):
    devices = came_ref.shape[0]
    came = jnp.transpose(came_ref[...])
    sub = old_ref.shape[1] // devices
    total = jnp.concatenate([came[i * 32 : i * 32 + ROWS] for i in range(sub)], axis=1)
    total_s[...] = jnp.zeros_like(total_s)
    pull_back(total, old_ref[...], camera_ref, total_s)
    for copy in range(out_ref.shape[0]):
        out_ref[copy] = total_s[...]


def adam_body(
    grads_ref, old_ref, order_ref, params_ref, moment1_ref, moment2_ref, full_ref, stack_s
):
    old = old_ref[...]
    grad = (grads_ref[0] + grads_ref[1]) + (grads_ref[2] + grads_ref[3])
    full_ref[0, 0] = (jnp.max(grad[10:11]) > 0.5).astype(jnp.int32)
    grad = grad[0:10]
    moment1 = 0.9 * old[10:20] + 0.1 * grad
    moment2 = 0.99 * old[24:34] + 0.01 * grad * grad
    stack_s[...] = jnp.zeros_like(stack_s)
    stack_s[0:10] = old[0:10] - 0.01 * moment1 / (jnp.sqrt(moment2) + 1e-08)
    stack_s[16:26] = moment1
    stack_s[32:42] = moment2
    new = dot(jnp.concatenate(parts(stack_s[...]), axis=0), order_ref[...])
    new = new[:48] + new[48:96] + new[96:]
    params_ref[...] = new[0:10]
    moment1_ref[...] = new[16:26]
    moment2_ref[...] = new[32:42]


def shape(*dims, dtype=F32):
    return jax.ShapeDtypeStruct(dims, dtype)


def exchange(x):
    devices = lax.axis_size("dev")
    parcel = x.reshape(devices, -1, 128)
    return lax.all_to_all(parcel, "dev", 0, 0, tiled=True).reshape(x.shape)


def share(copies):
    return lax.all_to_all(copies, "rep", 0, 0, tiled=True)


def local(params, moment1, moment2, camera, owner, local_index, target, rehome):
    devices = lax.axis_size("dev")
    reps = lax.axis_size("rep")
    gauss = params.shape[1]
    _, tiles, depth = local_index.shape
    entries = tiles * depth
    pix = target.shape[3]
    owners = owner.reshape(1, entries)
    ids = local_index[0]
    stack = pltpu.VMEM((32, gauss), F32)
    request, lists = call(
        request_body,
        (shape(devices, 128), shape(8, entries, dtype=jnp.int32)),
        [
            pltpu.VMEM((1, entries), jnp.int32), pltpu.VMEM((tiles, depth), jnp.int32),
            pltpu.VMEM((10, gauss), F32), pltpu.VMEM((1, devices), jnp.int32), stack,
            pltpu.VMEM((devices, 128), F32), pltpu.VMEM((8, entries), jnp.int32),
            pltpu.SemaphoreType.DMA((6,)),
        ],
        hbm=(0, 1, 2, 3),
        hbm_out=(0, 1),
        vmem=60 * 1024 * 1024,
    )(owners, ids, moment2, rehome)
    request = exchange(request)
    table, blocks, lists, goal, order = call(
        table_body,
        (
            shape(ROWS, gauss), shape(256 - VALUES * CAP, devices),
            shape(8, entries, dtype=jnp.int32), shape(3, tiles, pix),
            shape(gauss, gauss, dtype=BF16),
        ),
        [stack],
        smem=(2,),
    )(params, moment1, camera, lists, target[0].transpose(1, 0, 2))
    response = call(respond_body, shape(devices, 256), [pltpu.VMEM((256, devices), F32)])(
        request, table, blocks
    )
    response = exchange(response)
    plane = pltpu.VMEM((tiles * pix, depth), F32)
    images, grads, by_entry = call(
        composite_body,
        (shape(3, tiles, pix), shape(devices, 256), shape(ROWS, entries)),
        [
            plane, plane, plane, pltpu.VMEM((2, tiles * pix, depth), BF16),
            pltpu.VMEM((ROWS, entries), F32),
        ],
    )(response, lists, goal)
    grads = exchange(grads)
    grads, old = call(
        collect_body,
        (shape(reps, ROWS, gauss), shape(40, gauss)),
        [
            pltpu.VMEM((256, devices), F32), pltpu.VMEM((ROWS, gauss), F32),
            pltpu.SemaphoreType.DMA((reps,)),
        ],
        smem=(3,),
        hbm_out=(0,),
    )(grads, request, response, camera)
    update = call(
        adam_body,
        (shape(10, gauss),) * 3 + (shape(1, 1, dtype=jnp.int32),),
        [pltpu.VMEM((48, gauss), F32)],
        smem_out=(3,),
    )
    *out, full = update(share(grads), old, order)

    def by_owner(out, by_entry, lists, request, old, order, camera):
        sent = call(to_owner_body, shape(devices, 256))(by_entry, lists)
        sent = call(functools.partial(at_owner_body, gauss=gauss), shape(devices, 128))(
            exchange(sent), request, lists
        )
        sent = call(
            at_home_body, shape(reps, ROWS, gauss), [pltpu.VMEM((ROWS, gauss), F32)], smem=(2,)
        )(exchange(sent), old, camera)
        return list(update(share(sent), old, order)[:3])

    out = lax.cond(
        full[0, 0] > 0, by_owner, lambda out, *rest: out,
        list(out), by_entry, lists, request, old, order, camera,
    )
    return (*out, images.transpose(1, 0, 2)[None])


def solution(mesh):
    in_specs = (
        P(None, "dev"),
        P(None, "dev"),
        P(None, "dev"),
        P("rep", None),
        P("rep", "dev", None, None),
        P("rep", "dev", None),
        P("rep", "dev", None, None),
        P("dev", None),
    )
    out_specs = (P(None, "dev"), P(None, "dev"), P(None, "dev"), P("rep", "dev", None, None))
    return jax.shard_map(local, mesh=mesh, in_specs=in_specs, out_specs=out_specs, check_vma=False)
```

```python
import functools

import jax
import jax.numpy as jnp
from jax import lax
from jax.experimental import pallas as pl
from jax.experimental.pallas import tpu as pltpu
from jax.sharding import PartitionSpec as P

SIDE = 16
BACKGROUND = 0.5
CAP = 16
SUB = 4
HOME_CAP = 25
SENT = 10
VALUES = 10
UNROLL = 16
ROWS = 16
VMEM = 40 * 1024 * 1024
F32 = jnp.float32
BF16 = jnp.bfloat16


def one_hot(condition):
    return jnp.where(condition, 1.0, 0.0).astype(BF16)


def parts(x, count=3):
    out = []
    for _ in range(count):
        piece = x.astype(BF16)
        out.append(piece)
        x = x - piece.astype(F32)
    return out


def iota(shape, dim):
    return lax.broadcasted_iota(jnp.int32, shape, dim)


def dot(a, b):
    return lax.dot_general(a, b, (((1,), (0,)), ((), ())), preferred_element_type=F32)


def dot_t(a, b):
    return lax.dot_general(a, b, (((1,), (1,)), ((), ())), preferred_element_type=F32)


def call(body, out_shape, scratch=(), smem=(), hbm=(), smem_out=(), hbm_out=(), vmem=VMEM):
    def run(*args):
        space = [
            pltpu.SMEM if i in smem else pl.ANY if i in hbm else pltpu.VMEM
            for i in range(len(args))
        ]
        outs = jax.tree.map(lambda _: pl.BlockSpec(memory_space=pltpu.VMEM), out_shape)
        if smem_out or hbm_out:
            outs = tuple(
                pl.BlockSpec(
                    memory_space=pltpu.SMEM if i in smem_out else pl.ANY if i in hbm_out else pltpu.VMEM
                )
                for i in range(len(out_shape))
            )
        return pl.pallas_call(
            body,
            out_shape=out_shape,
            in_specs=[pl.BlockSpec(memory_space=m) for m in space],
            out_specs=outs,
            scratch_shapes=list(scratch),
            compiler_params=pltpu.CompilerParams(vmem_limit_bytes=vmem),
        )(*args)

    return run


def start(source, place, sem):
    copy = pltpu.make_async_copy(source, place, sem)
    copy.start()
    return copy


def along(ref):
    return jnp.concatenate([ref[t : t + 1] for t in range(ref.shape[0])], axis=1)


def rank_of(device, devices):
    entries = device.shape[1]
    step = 256
    before = one_hot(iota((step, step), 0) < iota((step, step), 1))
    steps = [device[:, start : start + step] for start in range(0, entries, step)]
    named = [jnp.where(iota((devices, step), 0) == d, 1.0, 0.0) for d in steps]
    count = dot(jnp.concatenate(named, axis=0).astype(BF16), before)
    base = jnp.zeros((devices, 1), F32)
    ranks = []
    for n, hot in enumerate(named):
        place = count[n * devices : (n + 1) * devices] + base
        base = base + jnp.sum(hot, axis=1, keepdims=True)
        ranks.append(jnp.sum(hot * place, axis=0, keepdims=True).astype(jnp.int32))
    return jnp.concatenate(ranks, axis=1), jnp.concatenate(named, axis=1).astype(BF16)


def homes_of(rehome_ref, gauss):
    devices = rehome_ref.shape[1]
    sub = gauss // devices
    homes = jnp.broadcast_to(rehome_ref[...].astype(F32), (8, devices)).astype(BF16)
    return dot(homes, one_hot(iota((devices, gauss), 1) // sub == iota((devices, gauss), 0)))[0:1]


def pack_blocks(stack, homes, devices, rows):
    gauss = stack.shape[1]
    sub = gauss // devices
    place = iota((devices, gauss), 0) == homes.astype(jnp.int32)
    within = iota((devices, gauss), 1) % sub
    pick = jnp.concatenate([one_hot(place & (within == i)) for i in range(sub)], axis=0)
    moved = dot_t(jnp.concatenate(parts(stack), axis=0), pick)
    moved = moved[:32] + moved[32:64] + moved[64:]
    moved = [moved[:rows, i * devices : (i + 1) * devices] for i in range(sub)]
    if sub * rows < 128:
        moved.append(jnp.zeros((128 - sub * rows, devices), F32))
    return jnp.transpose(jnp.concatenate(moved, axis=0))[:, : sub * rows]


def in_order(gauss, devices):
    sub = gauss // devices
    row = iota((gauss, gauss), 0)
    return one_hot(row % devices * sub + row // devices == iota((gauss, gauss), 1))


def sigmoid(x):
    return 1.0 / (1.0 + jnp.exp(-x))


def conics(rows):
    conic_a, conic_c, skew = jnp.exp(rows[3:4]), jnp.exp(rows[5:6]), jnp.tanh(rows[4:5])
    return conic_a, conic_c, skew, jnp.sqrt(conic_a * conic_c)


def request_body(
    owner_hbm, index_hbm, moment2_hbm, rehome_hbm,
    request_hbm, lists_hbm,
    owner_s, index_s, moment2_s, rehome_s, stack_s, request_s, lists_s, sems,
):
    copies = [
        start(source, place, sems.at[n])
        for n, (source, place) in enumerate(
            [
                (owner_hbm, owner_s), (index_hbm, index_s),
                (rehome_hbm, rehome_s), (moment2_hbm, moment2_s),
            ]
        )
    ]
    gauss = moment2_s.shape[1]
    devices = request_s.shape[0]
    stack_s[...] = jnp.zeros_like(stack_s)
    lists_s[...] = jnp.zeros_like(lists_s)
    for copy in copies:
        copy.wait()
    owner, ids = owner_s[...], along(index_s)
    rank, named = rank_of(owner, devices)
    homes = homes_of(rehome_s, gauss)
    lists_s[3:4, 0:gauss] = homes.astype(jnp.int32)
    lists_s[0:1] = owner
    lists_s[1:2] = ids
    lists_s[2:3] = rank
    kept = start(lists_s, lists_hbm, sems.at[4])
    slot = iota((CAP, ids.shape[1]), 0) == rank
    high = jnp.where(slot, (ids >> 4).astype(F32), 0.0)
    low = jnp.where(slot, (ids & 15).astype(F32), 0.0)
    total = dot_t(named, jnp.concatenate([high, low], axis=0).astype(BF16))
    asked = 16.0 * total[:, :CAP] + total[:, CAP:]
    stack_s[0:10] = moment2_s[...]
    blocks = pack_blocks(stack_s[...], homes, devices, 16)
    zero = jnp.zeros((devices, 128 - CAP - blocks.shape[1]), F32)
    request_s[...] = jnp.concatenate([blocks, asked, zero], axis=1)
    sent = start(request_s, request_hbm, sems.at[5])
    kept.wait()
    sent.wait()


def table_body(
    params_ref, moment1_ref, camera_ref, lists_ref, target_ref,
    table_ref, blocks_ref, kept_lists_ref, kept_target_ref, order_ref, stack_s,
):
    kept_lists_ref[...] = lists_ref[...]
    kept_target_ref[...] = target_ref[...]
    gauss = params_ref.shape[1]
    devices = blocks_ref.shape[1]
    cam = [camera_ref[0, i] for i in range(8)]
    homes = lists_ref[3:4, 0:gauss].astype(F32)
    order_ref[...] = in_order(gauss, devices)
    params = params_ref[...]
    stack_s[...] = jnp.zeros_like(stack_s)
    stack_s[0:10] = params
    stack_s[10:20] = moment1_ref[...]
    blocks = pack_blocks(stack_s[...], homes, devices, 24)
    zero = jnp.zeros((devices, 128 - blocks.shape[1]), F32)
    blocks = jnp.transpose(jnp.concatenate([blocks, zero], axis=1))
    blocks_ref[...] = blocks[: blocks_ref.shape[0]]
    x, y, z = params[0:1], params[1:2], params[2:3]
    conic_a, conic_c, skew, root = conics(params)
    table_ref[...] = jnp.zeros_like(table_ref)
    table_ref[0:1] = cam[0] * x + cam[1] * y + cam[2] * z + cam[3]
    table_ref[1:2] = cam[4] * x + cam[5] * y + cam[6] * z + cam[7]
    table_ref[2:3] = conic_a
    table_ref[3:4] = 0.9 * skew * root
    table_ref[4:5] = conic_c
    table_ref[5:9] = sigmoid(params[6:10])
    table_ref[9:10] = homes


def asked_hot(request_ref, gauss):
    devices = request_ref.shape[0]
    ids = jnp.transpose(request_ref[...])[64 : 64 + CAP].astype(jnp.int32)
    return jnp.concatenate(
        [one_hot(iota((gauss, devices), 0) == ids[j : j + 1]) for j in range(CAP)], axis=1
    )


def respond_body(request_ref, table_ref, blocks_ref, response_ref, out_s):
    devices = request_ref.shape[0]
    sub = table_ref.shape[1] // devices
    ids = jnp.transpose(request_ref[...])[64 : 64 + CAP].astype(jnp.int32)
    ids = jnp.concatenate([ids[j : j + 1] for j in range(CAP)], axis=1)
    hot = one_hot(iota((devices, ids.shape[1]), 0) == ids % devices)
    pieces = parts(table_ref[...])
    tables = [
        piece[:, i * devices : (i + 1) * devices] for piece in pieces for i in range(sub)
    ]
    all_got = dot(jnp.concatenate(tables, axis=0), hot)
    span = sub * ROWS
    all_got = all_got[:span] + all_got[span : 2 * span] + all_got[2 * span :]
    got = jnp.zeros((ROWS, ids.shape[1]), F32)
    for i in range(sub):
        got = got + jnp.where(ids // devices == i, all_got[i * ROWS : (i + 1) * ROWS], 0.0)
    for j in range(CAP):
        out_s[pl.ds(j, VALUES, stride=CAP), :] = got[:VALUES, j * devices : (j + 1) * devices]
    out_s[VALUES * CAP :] = blocks_ref[...]
    response_ref[:, :128] = jnp.transpose(out_s[:128])
    response_ref[:, 128:] = jnp.transpose(out_s[128:])


def settle(request_ref, response_ref, old_ref):
    devices = request_ref.shape[0]
    sub = old_ref.shape[1] // devices
    first = jnp.transpose(request_ref[...])
    second = jnp.transpose(response_ref[:, 128:])[VALUES * CAP - 128 :]
    for i in range(sub):
        cols = slice(i * devices, (i + 1) * devices)
        old_ref[0:24, cols] = second[i * 24 : i * 24 + 24]
        old_ref[24:40, cols] = first[i * 16 : i * 16 + 16]


def stacked(pieces):
    rows = [piece.astype(F32) for piece in pieces]
    return jnp.concatenate([*rows, jnp.zeros_like(rows[0])], axis=0).astype(BF16)


def groups(x):
    return x[0:8] + x[8:16] + x[16:24]


def composite_body(
    response_ref, lists_ref, target_ref,
    image_ref, grad_ref, entry_ref,
    alpha_s, run_s, slope_s, split_s, entry_s,
):
    devices = response_ref.shape[0]
    entries = lists_ref.shape[1]
    _, tiles, pix = target_ref.shape
    depth = entries // tiles
    owner, ids, rank = lists_ref[0:1], lists_ref[1:2], lists_ref[2:3]
    named = one_hot(iota((devices, entries), 0) == owner)
    got = jnp.concatenate(
        [jnp.transpose(response_ref[:, :128]), jnp.transpose(response_ref[:, 128:])], axis=0
    )[: VALUES * CAP]
    spread = dot(jnp.concatenate(parts(got), axis=0), named)
    span = VALUES * CAP
    spread = spread[:span] + spread[span : 2 * span] + spread[2 * span :]
    mine = iota((CAP, entries), 0) == rank
    values = [
        jnp.sum(jnp.where(mine, spread[r * CAP : (r + 1) * CAP], 0.0), axis=0, keepdims=True)
        for r in range(VALUES)
    ]
    screen_u, screen_v, conic_a, conic_b, conic_c, opacity = values[:6]
    entry_s[...] = jnp.zeros_like(entry_s)
    for c in range(3):
        entry_s[c : c + 1] = values[6 + c] - BACKGROUND
    colors = entry_s[0:8]
    peak, half_a, half_c = 0.99 * opacity, -0.5 * conic_a, -0.5 * conic_c
    across = iota((SIDE, depth), 0).astype(F32) - 7.5

    def chunk(t, i):
        return pl.ds(pl.multiple_of(t * pix + i * SIDE, SIDE), SIDE)

    def of(t):
        return slice(t * depth, (t + 1) * depth)

    def over_rows(body, init, t):
        return lax.fori_loop(0, pix // SIDE, functools.partial(body, t), init, unroll=UNROLL)

    def save(rows, x):
        for n, piece in enumerate(parts(x, 2)):
            split_s[n, rows] = piece

    for t in range(tiles):
        delta_u = across - screen_u[:, of(t)]
        first = half_a[:, of(t)] * delta_u * delta_u
        mixed = -conic_b[:, of(t)] * delta_u

        def forward(t, i, carry, first=first, mixed=mixed):
            rows = chunk(t, i)
            delta_v = (i.astype(F32) - 7.5) - screen_v[:, of(t)]
            power = first + delta_v * (mixed + half_c[:, of(t)] * delta_v)
            alpha = peak[:, of(t)] * jnp.exp(power)
            alpha_s[rows] = alpha
            save(rows, jnp.log(1.0 - alpha))
            return carry

        over_rows(forward, 0, t)
    half = depth // 2
    tri = one_hot(iota((half, half), 0) < iota((half, half), 1))
    full = jnp.ones((half, half), BF16)
    run_s[:, :half] = dot(split_s[0, :, :half], tri) + dot(split_s[1, :, :half], tri)
    run_s[:, half:] = (
        dot(split_s[0, :, half:], tri) + dot(split_s[1, :, half:], tri)
        + dot(split_s[0, :, :half], full) + dot(split_s[1, :, :half], full)
    )
    for t in range(tiles):

        def weigh(t, i, carry):
            rows = chunk(t, i)
            through = jnp.exp(run_s[rows])
            run_s[rows] = through
            save(rows, alpha_s[rows] * through)
            return carry

        over_rows(weigh, 0, t)
    color_grads = []
    for t in range(tiles):
        px = slice(t * pix, (t + 1) * pix)
        paints = parts(colors[:, of(t)])
        paint = stacked(paints)
        shown = groups(dot_t(paint, split_s[0, px]) + dot_t(paint, split_s[1, px]))
        shown = shown + BACKGROUND
        gaps = []
        for c in range(3):
            image_ref[c, t : t + 1] = shown[c : c + 1]
            gaps.append(shown[c : c + 1] - target_ref[c, t : t + 1])
        gap = jnp.concatenate([*gaps, jnp.zeros((5, pix), F32)], axis=0)
        gap_parts = parts(gap)
        drawn = stacked(gap_parts)
        color_grads.append(groups(dot(drawn, split_s[0, px]) + dot(drawn, split_s[1, px])))
        high, middle, low = [piece.astype(F32) for piece in gap_parts]
        left = jnp.concatenate(
            [high, high, high, middle, middle, low, jnp.zeros((80, pix), F32)], axis=0
        )
        left = jnp.concatenate(
            [jnp.transpose(left[:, :128]), jnp.transpose(left[:, 128:])], axis=0
        ).astype(BF16)
        high, middle, low = [piece.astype(F32) for piece in paints]
        right = jnp.concatenate(
            [high, middle, low, high, middle, high, jnp.zeros((80, depth), F32)], axis=0
        ).astype(BF16)
        slope_s[px] = dot(left, right)
    for t in range(tiles):

        def spread_back(t, i, carry):
            rows = chunk(t, i)
            through_slope = run_s[rows] * slope_s[rows]
            slope_s[rows] = through_slope
            save(rows, alpha_s[rows] * through_slope)
            return carry

        over_rows(spread_back, 0, t)
    tri = one_hot(iota((half, half), 0) > iota((half, half), 1))
    run_s[:, half:] = dot(split_s[0, :, half:], tri) + dot(split_s[1, :, half:], tri)
    run_s[:, :half] = (
        dot(split_s[0, :, :half], tri) + dot(split_s[1, :, :half], tri)
        + dot(split_s[0, :, half:], full) + dot(split_s[1, :, half:], full)
    )
    sums = []
    for t in range(tiles):

        def backward(t, i, sums):
            rows = chunk(t, i)
            alpha = alpha_s[rows]
            pull = alpha * (slope_s[rows] - run_s[rows] / (1.0 - alpha))
            delta_v = (i.astype(F32) - 7.5) - screen_v[:, of(t)]
            pull_v = pull * delta_v
            return sums[0] + pull, sums[1] + pull_v, sums[2] + pull_v * delta_v

        zero = jnp.zeros((SIDE, depth), F32)
        plain, with_v, with_vv = over_rows(backward, (zero, zero, zero), t)
        delta_u = across - screen_u[:, of(t)]
        plain_u = plain * delta_u
        sums.append(
            [
                jnp.sum(a, axis=0, keepdims=True)
                for a in (plain, plain_u, with_v, plain_u * delta_u, with_v * delta_u, with_vv)
            ]
        )
    s_0, s_u, s_v, s_uu, s_uv, s_vv = [
        jnp.concatenate([s[n] for s in sums], axis=1) for n in range(6)
    ]
    entry_s[0:1] = conic_a * s_u + conic_b * s_v
    entry_s[1:2] = conic_b * s_u + conic_c * s_v
    entry_s[2:3] = -0.5 * s_uu
    entry_s[3:4] = -s_uv
    entry_s[4:5] = -0.5 * s_vv
    entry_s[5:6] = s_0 / opacity
    entry_s[6:9] = jnp.concatenate(color_grads, axis=1)[0:3]
    entry_s[9:10] = (owner * SUB + ids % SUB).astype(F32)
    grads = entry_s[...]
    entry_ref[...] = grads
    home = (values[9] + 0.5).astype(jnp.int32)
    order, moves = rank_of(home, devices)
    lanes = grad_ref.shape[1]
    row = iota((8, entries), 0)
    pieces = [piece.astype(F32) for piece in parts(grads, 2)]
    sent = [[], []]
    for start_row in range(0, lanes, 8):
        c, last = start_row // HOME_CAP, (start_row + 7) // HOME_CAP
        here = row == order - (start_row - c * HOME_CAP)
        if last > c:
            first = row < last * HOME_CAP - start_row
            here = (here & first) | (row == order - (start_row - last * HOME_CAP))
        for n in range(2):
            value = pieces[n][c : c + 1]
            if last > c:
                value = jnp.where(first, value, pieces[n][last : last + 1])
            sent[n].append(jnp.where(here, value, 0.0))
    sent = [jnp.concatenate(rows, axis=0).astype(BF16) for rows in sent]
    sent = dot_t(jnp.concatenate(sent, axis=0), moves)
    sent = sent[:lanes] + sent[lanes:]
    sent = jnp.concatenate([jnp.transpose(sent[:128]), jnp.transpose(sent[128:])], axis=1)
    over = jnp.max(order, axis=1, keepdims=True) >= HOME_CAP
    flag = jnp.where(over, 1.0, 0.0)
    grad_ref[...] = jnp.where(iota((devices, lanes), 1) < SENT * HOME_CAP, sent, flag)


def pull_back(total, old, camera_ref, out_ref):
    cam = [camera_ref[0, i] for i in range(8)]
    g_u, g_v, g_a, g_b, g_c = [total[r : r + 1] for r in range(5)]
    conic_a, conic_c, skew, root = conics(old)
    half_b = g_b * (0.45 * skew * root)
    level = sigmoid(old[6:10])
    out_ref[0:1] = cam[0] * g_u + cam[4] * g_v
    out_ref[1:2] = cam[1] * g_u + cam[5] * g_v
    out_ref[2:3] = cam[2] * g_u + cam[6] * g_v
    out_ref[3:4] = g_a * conic_a + half_b
    out_ref[4:5] = g_b * 0.9 * (1.0 - skew * skew) * root
    out_ref[5:6] = g_c * conic_c + half_b
    out_ref[6:10] = total[5:9] * level * (1.0 - level)


def collect_body(
    grad_ref, request_ref, response_ref, camera_ref, out_hbm, old_ref, came_s, total_s, sems
):
    settle(request_ref, response_ref, old_ref)
    devices = grad_ref.shape[0]
    sub = old_ref.shape[1] // devices
    came_s[:128] = jnp.transpose(grad_ref[:, :128])
    came_s[128:] = jnp.transpose(grad_ref[:, 128:])
    spots = (came_s[9 * HOME_CAP : 10 * HOME_CAP] + 0.5).astype(jnp.int32)
    blocks, places = spots // sub, spots % sub
    hot, came = [], []
    zero = jnp.zeros((6, devices), F32)
    for j in range(HOME_CAP):
        hot.append(one_hot(iota((devices, devices), 0) == blocks[j : j + 1]))
        slot = jnp.concatenate([came_s[pl.ds(j, SENT, stride=HOME_CAP), :], zero], axis=0)
        place = places[j : j + 1]
        came.append(
            jnp.concatenate([jnp.where(place == i, slot, 0.0) for i in range(sub)], axis=0)
        )
    came = parts(jnp.concatenate(came, axis=1), 2)
    total = dot_t(jnp.concatenate(came, axis=0), jnp.concatenate(hot, axis=1))
    total = total[: sub * ROWS] + total[sub * ROWS :]
    total = jnp.concatenate([total[i * ROWS : (i + 1) * ROWS] for i in range(sub)], axis=1)
    total_s[...] = jnp.zeros_like(total_s)
    pull_back(total, old_ref[...], camera_ref, total_s)
    flags = came_s[SENT * HOME_CAP :]
    flag = jnp.max(jnp.max(flags, axis=1, keepdims=True), axis=0, keepdims=True)
    total_s[10:11] = flag + jnp.zeros((1, total_s.shape[1]), F32)
    copies = [start(total_s, out_hbm.at[n], sems.at[n]) for n in range(out_hbm.shape[0])]
    for copy in copies:
        copy.wait()


def to_owner_body(entry_ref, lists_ref, out_ref):
    devices = out_ref.shape[0]
    rank = lists_ref[2:3]
    named = one_hot(iota((devices, rank.shape[1]), 0) == lists_ref[0:1])
    grads = entry_ref[...]
    slots = jnp.concatenate([jnp.where(rank == j, grads, 0.0) for j in range(CAP)], axis=0)
    sent = sum(dot_t(piece, named) for piece in parts(slots))
    out_ref[:, :128] = jnp.transpose(sent[:128])
    out_ref[:, 128:] = jnp.transpose(sent[128:])


def at_owner_body(grad_ref, request_ref, lists_ref, out_ref, *, gauss):
    devices = grad_ref.shape[0]
    came = jnp.concatenate(
        [jnp.transpose(grad_ref[:, :128]), jnp.transpose(grad_ref[:, 128:])], axis=0
    )
    came = jnp.concatenate([came[j * ROWS : (j + 1) * ROWS] for j in range(CAP)], axis=1)
    total = dot_t(jnp.concatenate(parts(came), axis=0), asked_hot(request_ref, gauss))
    total = total[:ROWS] + total[ROWS : 2 * ROWS] + total[2 * ROWS :]
    stack = jnp.concatenate([total, jnp.zeros_like(total)], axis=0)
    out_ref[...] = pack_blocks(stack, lists_ref[3:4, 0:gauss].astype(F32), devices, 32)


def at_home_body(came_ref, old_ref, camera_ref, out_ref, total_s):
    devices = came_ref.shape[0]
    came = jnp.transpose(came_ref[...])
    sub = old_ref.shape[1] // devices
    total = jnp.concatenate([came[i * 32 : i * 32 + ROWS] for i in range(sub)], axis=1)
    total_s[...] = jnp.zeros_like(total_s)
    pull_back(total, old_ref[...], camera_ref, total_s)
    for copy in range(out_ref.shape[0]):
        out_ref[copy] = total_s[...]


def adam_body(
    grads_ref, old_ref, order_ref, params_ref, moment1_ref, moment2_ref, full_ref, stack_s
):
    old = old_ref[...]
    grad = (grads_ref[0] + grads_ref[1]) + (grads_ref[2] + grads_ref[3])
    full_ref[0, 0] = (jnp.max(grad[10:11]) > 0.5).astype(jnp.int32)
    grad = grad[0:10]
    moment1 = 0.9 * old[10:20] + 0.1 * grad
    moment2 = 0.99 * old[24:34] + 0.01 * grad * grad
    stack_s[...] = jnp.zeros_like(stack_s)
    stack_s[0:10] = old[0:10] - 0.01 * moment1 / (jnp.sqrt(moment2) + 1e-08)
    stack_s[16:26] = moment1
    stack_s[32:42] = moment2
    new = dot(jnp.concatenate(parts(stack_s[...]), axis=0), order_ref[...])
    new = new[:48] + new[48:96] + new[96:]
    params_ref[...] = new[0:10]
    moment1_ref[...] = new[16:26]
    moment2_ref[...] = new[32:42]


def shape(*dims, dtype=F32):
    return jax.ShapeDtypeStruct(dims, dtype)


def exchange(x):
    devices = lax.axis_size("dev")
    parcel = x.reshape(devices, -1, 128)
    return lax.all_to_all(parcel, "dev", 0, 0, tiled=True).reshape(x.shape)


def share(copies):
    return lax.all_to_all(copies, "rep", 0, 0, tiled=True)


def local(params, moment1, moment2, camera, owner, local_index, target, rehome):
    devices = lax.axis_size("dev")
    reps = lax.axis_size("rep")
    gauss = params.shape[1]
    _, tiles, depth = local_index.shape
    entries = tiles * depth
    pix = target.shape[3]
    owners = owner.reshape(1, entries)
    ids = local_index[0]
    stack = pltpu.VMEM((32, gauss), F32)
    request, lists = call(
        request_body,
        (shape(devices, 128), shape(8, entries, dtype=jnp.int32)),
        [
            pltpu.VMEM((1, entries), jnp.int32), pltpu.VMEM((tiles, depth), jnp.int32),
            pltpu.VMEM((10, gauss), F32), pltpu.VMEM((1, devices), jnp.int32), stack,
            pltpu.VMEM((devices, 128), F32), pltpu.VMEM((8, entries), jnp.int32),
            pltpu.SemaphoreType.DMA((6,)),
        ],
        hbm=(0, 1, 2, 3),
        hbm_out=(0, 1),
        vmem=60 * 1024 * 1024,
    )(owners, ids, moment2, rehome)
    request = exchange(request)
    table, blocks, lists, goal, order = call(
        table_body,
        (
            shape(ROWS, gauss), shape(256 - VALUES * CAP, devices),
            shape(8, entries, dtype=jnp.int32), shape(3, tiles, pix),
            shape(gauss, gauss, dtype=BF16),
        ),
        [stack],
        smem=(2,),
    )(params, moment1, camera, lists, target[0].transpose(1, 0, 2))
    response = call(respond_body, shape(devices, 256), [pltpu.VMEM((256, devices), F32)])(
        request, table, blocks
    )
    response = exchange(response)
    plane = pltpu.VMEM((tiles * pix, depth), F32)
    images, grads, by_entry = call(
        composite_body,
        (shape(3, tiles, pix), shape(devices, 256), shape(ROWS, entries)),
        [
            plane, plane, plane, pltpu.VMEM((2, tiles * pix, depth), BF16),
            pltpu.VMEM((ROWS, entries), F32),
        ],
    )(response, lists, goal)
    grads = exchange(grads)
    grads, old = call(
        collect_body,
        (shape(reps, ROWS, gauss), shape(40, gauss)),
        [
            pltpu.VMEM((256, devices), F32), pltpu.VMEM((ROWS, gauss), F32),
            pltpu.SemaphoreType.DMA((reps,)),
        ],
        smem=(3,),
        hbm_out=(0,),
    )(grads, request, response, camera)
    update = call(
        adam_body,
        (shape(10, gauss),) * 3 + (shape(1, 1, dtype=jnp.int32),),
        [pltpu.VMEM((48, gauss), F32)],
        smem_out=(3,),
    )
    *out, full = update(share(grads), old, order)

    def by_owner(out, by_entry, lists, request, old, order, camera):
        sent = call(to_owner_body, shape(devices, 256))(by_entry, lists)
        sent = call(functools.partial(at_owner_body, gauss=gauss), shape(devices, 128))(
            exchange(sent), request, lists
        )
        sent = call(
            at_home_body, shape(reps, ROWS, gauss), [pltpu.VMEM((ROWS, gauss), F32)], smem=(2,)
        )(exchange(sent), old, camera)
        return list(update(share(sent), old, order)[:3])

    _, out = lax.while_loop(
        lambda carry: carry[0] > 0,
        lambda carry: (
            jnp.int32(0), by_owner(carry[1], by_entry, lists, request, old, order, camera)
        ),
        (full[0, 0], list(out)),
    )
    return (*out, images.transpose(1, 0, 2)[None])


def solution(mesh):
    in_specs = (
        P(None, "dev"),
        P(None, "dev"),
        P(None, "dev"),
        P("rep", None),
        P("rep", "dev", None, None),
        P("rep", "dev", None),
        P("rep", "dev", None, None),
        P("dev", None),
    )
    out_specs = (P(None, "dev"), P(None, "dev"), P(None, "dev"), P("rep", "dev", None, None))
    return jax.shard_map(local, mesh=mesh, in_specs=in_specs, out_specs=out_specs, check_vma=False)
```

```python
import functools

import jax
import jax.numpy as jnp
from jax import lax
from jax.experimental import pallas as pl
from jax.experimental.pallas import tpu as pltpu
from jax.sharding import PartitionSpec as P

SIDE = 16
BACKGROUND = 0.5
CAP = 16
SUB = 4
HOME_CAP = 25
SENT = 10
VALUES = 10
UNROLL = 16
ROWS = 16
VMEM = 40 * 1024 * 1024
F32 = jnp.float32
BF16 = jnp.bfloat16


def one_hot(condition):
    return jnp.where(condition, 1.0, 0.0).astype(BF16)


def parts(x, count=3):
    out = []
    for _ in range(count):
        piece = x.astype(BF16)
        out.append(piece)
        x = x - piece.astype(F32)
    return out


def iota(shape, dim):
    return lax.broadcasted_iota(jnp.int32, shape, dim)


def dot(a, b):
    return lax.dot_general(a, b, (((1,), (0,)), ((), ())), preferred_element_type=F32)


def dot_t(a, b):
    return lax.dot_general(a, b, (((1,), (1,)), ((), ())), preferred_element_type=F32)


def call(body, out_shape, scratch=(), smem=(), hbm=(), smem_out=(), hbm_out=(), vmem=VMEM):
    def run(*args):
        space = [
            pltpu.SMEM if i in smem else pl.ANY if i in hbm else pltpu.VMEM
            for i in range(len(args))
        ]
        outs = jax.tree.map(lambda _: pl.BlockSpec(memory_space=pltpu.VMEM), out_shape)
        if smem_out or hbm_out:
            outs = tuple(
                pl.BlockSpec(
                    memory_space=pltpu.SMEM if i in smem_out else pl.ANY if i in hbm_out else pltpu.VMEM
                )
                for i in range(len(out_shape))
            )
        return pl.pallas_call(
            body,
            out_shape=out_shape,
            in_specs=[pl.BlockSpec(memory_space=m) for m in space],
            out_specs=outs,
            scratch_shapes=list(scratch),
            compiler_params=pltpu.CompilerParams(vmem_limit_bytes=vmem),
        )(*args)

    return run


def start(source, place, sem):
    copy = pltpu.make_async_copy(source, place, sem)
    copy.start()
    return copy


def along(ref):
    return jnp.concatenate([ref[t : t + 1] for t in range(ref.shape[0])], axis=1)


def rank_of(device, devices):
    entries = device.shape[1]
    step = 256
    before = one_hot(iota((step, step), 0) < iota((step, step), 1))
    steps = [device[:, start : start + step] for start in range(0, entries, step)]
    named = [jnp.where(iota((devices, step), 0) == d, 1.0, 0.0) for d in steps]
    count = dot(jnp.concatenate(named, axis=0).astype(BF16), before)
    base = jnp.zeros((devices, 1), F32)
    ranks = []
    for n, hot in enumerate(named):
        place = count[n * devices : (n + 1) * devices] + base
        base = base + jnp.sum(hot, axis=1, keepdims=True)
        ranks.append(jnp.sum(hot * place, axis=0, keepdims=True).astype(jnp.int32))
    return jnp.concatenate(ranks, axis=1), jnp.concatenate(named, axis=1).astype(BF16)


def homes_of(rehome_ref, gauss):
    devices = rehome_ref.shape[1]
    sub = gauss // devices
    homes = jnp.broadcast_to(rehome_ref[...].astype(F32), (8, devices)).astype(BF16)
    return dot(homes, one_hot(iota((devices, gauss), 1) // sub == iota((devices, gauss), 0)))[0:1]


def pack_blocks(stack, homes, devices, rows):
    gauss = stack.shape[1]
    sub = gauss // devices
    place = iota((devices, gauss), 0) == homes.astype(jnp.int32)
    within = iota((devices, gauss), 1) % sub
    pick = jnp.concatenate([one_hot(place & (within == i)) for i in range(sub)], axis=0)
    moved = dot_t(jnp.concatenate(parts(stack), axis=0), pick)
    moved = moved[:32] + moved[32:64] + moved[64:]
    moved = [moved[:rows, i * devices : (i + 1) * devices] for i in range(sub)]
    if sub * rows < 128:
        moved.append(jnp.zeros((128 - sub * rows, devices), F32))
    return jnp.transpose(jnp.concatenate(moved, axis=0))[:, : sub * rows]


def in_order(gauss, devices):
    sub = gauss // devices
    row = iota((gauss, gauss), 0)
    return one_hot(row % devices * sub + row // devices == iota((gauss, gauss), 1))


def sigmoid(x):
    return 1.0 / (1.0 + jnp.exp(-x))


def conics(rows):
    conic_a, conic_c, skew = jnp.exp(rows[3:4]), jnp.exp(rows[5:6]), jnp.tanh(rows[4:5])
    return conic_a, conic_c, skew, jnp.sqrt(conic_a * conic_c)


def request_body(
    owner_hbm, index_hbm, moment2_hbm, rehome_hbm,
    request_hbm, lists_hbm,
    owner_s, index_s, moment2_s, rehome_s, stack_s, request_s, lists_s, sems,
):
    copies = [
        start(source, place, sems.at[n])
        for n, (source, place) in enumerate(
            [
                (owner_hbm, owner_s), (index_hbm, index_s),
                (rehome_hbm, rehome_s), (moment2_hbm, moment2_s),
            ]
        )
    ]
    gauss = moment2_s.shape[1]
    devices = request_s.shape[0]
    stack_s[...] = jnp.zeros_like(stack_s)
    lists_s[...] = jnp.zeros_like(lists_s)
    for copy in copies:
        copy.wait()
    owner, ids = owner_s[...], along(index_s)
    rank, named = rank_of(owner, devices)
    homes = homes_of(rehome_s, gauss)
    lists_s[3:4, 0:gauss] = homes.astype(jnp.int32)
    lists_s[0:1] = owner
    lists_s[1:2] = ids
    lists_s[2:3] = rank
    kept = start(lists_s, lists_hbm, sems.at[4])
    slot = iota((CAP, ids.shape[1]), 0) == rank
    high = jnp.where(slot, (ids >> 4).astype(F32), 0.0)
    low = jnp.where(slot, (ids & 15).astype(F32), 0.0)
    total = dot_t(named, jnp.concatenate([high, low], axis=0).astype(BF16))
    asked = 16.0 * total[:, :CAP] + total[:, CAP:]
    stack_s[0:10] = moment2_s[...]
    blocks = pack_blocks(stack_s[...], homes, devices, 16)
    zero = jnp.zeros((devices, 128 - CAP - blocks.shape[1]), F32)
    request_s[...] = jnp.concatenate([blocks, asked, zero], axis=1)
    sent = start(request_s, request_hbm, sems.at[5])
    kept.wait()
    sent.wait()


def table_body(
    params_ref, moment1_ref, camera_ref, lists_ref, target_ref,
    table_ref, blocks_ref, kept_lists_ref, kept_target_ref, order_ref, stack_s,
):
    kept_lists_ref[...] = lists_ref[...]
    kept_target_ref[...] = target_ref[...]
    gauss = params_ref.shape[1]
    devices = blocks_ref.shape[1]
    cam = [camera_ref[0, i] for i in range(8)]
    homes = lists_ref[3:4, 0:gauss].astype(F32)
    order_ref[...] = in_order(gauss, devices)
    params = params_ref[...]
    stack_s[...] = jnp.zeros_like(stack_s)
    stack_s[0:10] = params
    stack_s[10:20] = moment1_ref[...]
    blocks = pack_blocks(stack_s[...], homes, devices, 24)
    zero = jnp.zeros((devices, 128 - blocks.shape[1]), F32)
    blocks = jnp.transpose(jnp.concatenate([blocks, zero], axis=1))
    blocks_ref[...] = blocks[: blocks_ref.shape[0]]
    x, y, z = params[0:1], params[1:2], params[2:3]
    conic_a, conic_c, skew, root = conics(params)
    table_ref[...] = jnp.zeros_like(table_ref)
    table_ref[0:1] = cam[0] * x + cam[1] * y + cam[2] * z + cam[3]
    table_ref[1:2] = cam[4] * x + cam[5] * y + cam[6] * z + cam[7]
    table_ref[2:3] = conic_a
    table_ref[3:4] = 0.9 * skew * root
    table_ref[4:5] = conic_c
    table_ref[5:9] = sigmoid(params[6:10])
    table_ref[9:10] = homes


def asked_hot(request_ref, gauss):
    devices = request_ref.shape[0]
    ids = jnp.transpose(request_ref[...])[64 : 64 + CAP].astype(jnp.int32)
    return jnp.concatenate(
        [one_hot(iota((gauss, devices), 0) == ids[j : j + 1]) for j in range(CAP)], axis=1
    )


def respond_body(request_ref, table_ref, blocks_ref, response_ref, out_s):
    devices = request_ref.shape[0]
    sub = table_ref.shape[1] // devices
    ids = jnp.transpose(request_ref[...])[64 : 64 + CAP].astype(jnp.int32)
    ids = jnp.concatenate([ids[j : j + 1] for j in range(CAP)], axis=1)
    hot = one_hot(iota((devices, ids.shape[1]), 0) == ids % devices)
    pieces = parts(table_ref[...])
    tables = [
        piece[:, i * devices : (i + 1) * devices] for piece in pieces for i in range(sub)
    ]
    all_got = dot(jnp.concatenate(tables, axis=0), hot)
    span = sub * ROWS
    all_got = all_got[:span] + all_got[span : 2 * span] + all_got[2 * span :]
    got = jnp.zeros((ROWS, ids.shape[1]), F32)
    for i in range(sub):
        got = got + jnp.where(ids // devices == i, all_got[i * ROWS : (i + 1) * ROWS], 0.0)
    for j in range(CAP):
        out_s[pl.ds(j, VALUES, stride=CAP), :] = got[:VALUES, j * devices : (j + 1) * devices]
    out_s[VALUES * CAP :] = blocks_ref[...]
    response_ref[:, :128] = jnp.transpose(out_s[:128])
    response_ref[:, 128:] = jnp.transpose(out_s[128:])


def settle(request_ref, response_ref, old_ref):
    devices = request_ref.shape[0]
    sub = old_ref.shape[1] // devices
    first = jnp.transpose(request_ref[...])
    second = jnp.transpose(response_ref[:, 128:])[VALUES * CAP - 128 :]
    for i in range(sub):
        cols = slice(i * devices, (i + 1) * devices)
        old_ref[0:24, cols] = second[i * 24 : i * 24 + 24]
        old_ref[24:40, cols] = first[i * 16 : i * 16 + 16]


def stacked(pieces):
    rows = [piece.astype(F32) for piece in pieces]
    return jnp.concatenate([*rows, jnp.zeros_like(rows[0])], axis=0).astype(BF16)


def groups(x):
    return x[0:8] + x[8:16] + x[16:24]


def composite_body(
    response_ref, lists_ref, target_ref,
    image_ref, grad_ref, entry_ref,
    alpha_s, run_s, slope_s, split_s, entry_s,
):
    devices = response_ref.shape[0]
    entries = lists_ref.shape[1]
    _, tiles, pix = target_ref.shape
    depth = entries // tiles
    owner, ids, rank = lists_ref[0:1], lists_ref[1:2], lists_ref[2:3]
    named = one_hot(iota((devices, entries), 0) == owner)
    got = jnp.concatenate(
        [jnp.transpose(response_ref[:, :128]), jnp.transpose(response_ref[:, 128:])], axis=0
    )[: VALUES * CAP]
    spread = dot(jnp.concatenate(parts(got), axis=0), named)
    span = VALUES * CAP
    spread = spread[:span] + spread[span : 2 * span] + spread[2 * span :]
    mine = iota((CAP, entries), 0) == rank
    values = [
        jnp.sum(jnp.where(mine, spread[r * CAP : (r + 1) * CAP], 0.0), axis=0, keepdims=True)
        for r in range(VALUES)
    ]
    screen_u, screen_v, conic_a, conic_b, conic_c, opacity = values[:6]
    entry_s[...] = jnp.zeros_like(entry_s)
    for c in range(3):
        entry_s[c : c + 1] = values[6 + c] - BACKGROUND
    colors = entry_s[0:8]
    peak, half_a, half_c = 0.99 * opacity, -0.5 * conic_a, -0.5 * conic_c
    across = iota((SIDE, depth), 0).astype(F32) - 7.5

    def chunk(t, i):
        return pl.ds(pl.multiple_of(t * pix + i * SIDE, SIDE), SIDE)

    def of(t):
        return slice(t * depth, (t + 1) * depth)

    def over_rows(body, init, t):
        return lax.fori_loop(0, pix // SIDE, functools.partial(body, t), init, unroll=UNROLL)

    def save(rows, x):
        for n, piece in enumerate(parts(x, 2)):
            split_s[n, rows] = piece

    for t in range(tiles):
        delta_u = across - screen_u[:, of(t)]
        first = half_a[:, of(t)] * delta_u * delta_u
        mixed = -conic_b[:, of(t)] * delta_u

        def forward(t, i, carry, first=first, mixed=mixed):
            rows = chunk(t, i)
            delta_v = (i.astype(F32) - 7.5) - screen_v[:, of(t)]
            power = first + delta_v * (mixed + half_c[:, of(t)] * delta_v)
            alpha = peak[:, of(t)] * jnp.exp(power)
            alpha_s[rows] = alpha
            save(rows, jnp.log(1.0 - alpha))
            return carry

        over_rows(forward, 0, t)
    half = depth // 2
    tri = one_hot(iota((half, half), 0) < iota((half, half), 1))
    full = jnp.ones((half, half), BF16)
    run_s[:, :half] = dot(split_s[0, :, :half], tri) + dot(split_s[1, :, :half], tri)
    run_s[:, half:] = (
        dot(split_s[0, :, half:], tri) + dot(split_s[1, :, half:], tri)
        + dot(split_s[0, :, :half], full) + dot(split_s[1, :, :half], full)
    )
    for t in range(tiles):

        def weigh(t, i, carry):
            rows = chunk(t, i)
            through = jnp.exp(run_s[rows])
            run_s[rows] = through
            save(rows, alpha_s[rows] * through)
            return carry

        over_rows(weigh, 0, t)
    color_grads = []
    for t in range(tiles):
        px = slice(t * pix, (t + 1) * pix)
        paints = parts(colors[:, of(t)])
        paint = stacked(paints)
        shown = groups(dot_t(paint, split_s[0, px]) + dot_t(paint, split_s[1, px]))
        shown = shown + BACKGROUND
        gaps = []
        for c in range(3):
            image_ref[c, t : t + 1] = shown[c : c + 1]
            gaps.append(shown[c : c + 1] - target_ref[c, t : t + 1])
        gap = jnp.concatenate([*gaps, jnp.zeros((5, pix), F32)], axis=0)
        gap_parts = parts(gap)
        drawn = stacked(gap_parts)
        color_grads.append(groups(dot(drawn, split_s[0, px]) + dot(drawn, split_s[1, px])))
        high, middle, low = [piece.astype(F32) for piece in gap_parts]
        left = jnp.concatenate(
            [high, high, high, middle, middle, low, jnp.zeros((80, pix), F32)], axis=0
        )
        left = jnp.concatenate(
            [jnp.transpose(left[:, :128]), jnp.transpose(left[:, 128:])], axis=0
        ).astype(BF16)
        high, middle, low = [piece.astype(F32) for piece in paints]
        right = jnp.concatenate(
            [high, middle, low, high, middle, high, jnp.zeros((80, depth), F32)], axis=0
        ).astype(BF16)
        slope_s[px] = dot(left, right)
    for t in range(tiles):

        def spread_back(t, i, carry):
            rows = chunk(t, i)
            through_slope = run_s[rows] * slope_s[rows]
            slope_s[rows] = through_slope
            save(rows, alpha_s[rows] * through_slope)
            return carry

        over_rows(spread_back, 0, t)
    tri = one_hot(iota((half, half), 0) > iota((half, half), 1))
    run_s[:, half:] = dot(split_s[0, :, half:], tri) + dot(split_s[1, :, half:], tri)
    run_s[:, :half] = (
        dot(split_s[0, :, :half], tri) + dot(split_s[1, :, :half], tri)
        + dot(split_s[0, :, half:], full) + dot(split_s[1, :, half:], full)
    )
    sums = []
    for t in range(tiles):

        def backward(t, i, sums):
            rows = chunk(t, i)
            alpha = alpha_s[rows]
            pull = alpha * (slope_s[rows] - run_s[rows] / (1.0 - alpha))
            delta_v = (i.astype(F32) - 7.5) - screen_v[:, of(t)]
            pull_v = pull * delta_v
            return sums[0] + pull, sums[1] + pull_v, sums[2] + pull_v * delta_v

        zero = jnp.zeros((SIDE, depth), F32)
        plain, with_v, with_vv = over_rows(backward, (zero, zero, zero), t)
        delta_u = across - screen_u[:, of(t)]
        plain_u = plain * delta_u
        sums.append(
            [
                jnp.sum(a, axis=0, keepdims=True)
                for a in (plain, plain_u, with_v, plain_u * delta_u, with_v * delta_u, with_vv)
            ]
        )
    s_0, s_u, s_v, s_uu, s_uv, s_vv = [
        jnp.concatenate([s[n] for s in sums], axis=1) for n in range(6)
    ]
    entry_s[0:1] = conic_a * s_u + conic_b * s_v
    entry_s[1:2] = conic_b * s_u + conic_c * s_v
    entry_s[2:3] = -0.5 * s_uu
    entry_s[3:4] = -s_uv
    entry_s[4:5] = -0.5 * s_vv
    entry_s[5:6] = s_0 / opacity
    entry_s[6:9] = jnp.concatenate(color_grads, axis=1)[0:3]
    entry_s[9:10] = (owner * SUB + ids % SUB).astype(F32)
    grads = entry_s[...]
    entry_ref[...] = grads
    home = (values[9] + 0.5).astype(jnp.int32)
    order, moves = rank_of(home, devices)
    lanes = grad_ref.shape[1]
    row = iota((8, entries), 0)
    pieces = [piece.astype(F32) for piece in parts(grads, 2)]
    sent = [[], []]
    for start_row in range(0, lanes, 8):
        c, last = start_row // HOME_CAP, (start_row + 7) // HOME_CAP
        here = row == order - (start_row - c * HOME_CAP)
        if last > c:
            first = row < last * HOME_CAP - start_row
            here = (here & first) | (row == order - (start_row - last * HOME_CAP))
        for n in range(2):
            value = pieces[n][c : c + 1]
            if last > c:
                value = jnp.where(first, value, pieces[n][last : last + 1])
            sent[n].append(jnp.where(here, value, 0.0))
    sent = [jnp.concatenate(rows, axis=0).astype(BF16) for rows in sent]
    sent = dot_t(jnp.concatenate(sent, axis=0), moves)
    sent = sent[:lanes] + sent[lanes:]
    sent = jnp.concatenate([jnp.transpose(sent[:128]), jnp.transpose(sent[128:])], axis=1)
    over = jnp.max(order, axis=1, keepdims=True) >= HOME_CAP
    flag = jnp.where(over, 1.0, 0.0)
    grad_ref[...] = jnp.where(iota((devices, lanes), 1) < SENT * HOME_CAP, sent, flag)


def pull_back(total, old, camera_ref, out_ref):
    cam = [camera_ref[0, i] for i in range(8)]
    g_u, g_v, g_a, g_b, g_c = [total[r : r + 1] for r in range(5)]
    conic_a, conic_c, skew, root = conics(old)
    half_b = g_b * (0.45 * skew * root)
    level = sigmoid(old[6:10])
    out_ref[0:1] = cam[0] * g_u + cam[4] * g_v
    out_ref[1:2] = cam[1] * g_u + cam[5] * g_v
    out_ref[2:3] = cam[2] * g_u + cam[6] * g_v
    out_ref[3:4] = g_a * conic_a + half_b
    out_ref[4:5] = g_b * 0.9 * (1.0 - skew * skew) * root
    out_ref[5:6] = g_c * conic_c + half_b
    out_ref[6:10] = total[5:9] * level * (1.0 - level)


def spread_copies(total_s, out_ref):
    total = total_s[0:12]
    for copy in range(out_ref.shape[0]):
        for i in range(total.shape[1] // 128):
            out_ref[copy, i * 12 : i * 12 + 12] = total[:, i * 128 : i * 128 + 128]


def collect_body(
    grad_ref, request_ref, response_ref, camera_ref, out_ref, old_ref, came_s, total_s
):
    settle(request_ref, response_ref, old_ref)
    devices = grad_ref.shape[0]
    sub = old_ref.shape[1] // devices
    came_s[:128] = jnp.transpose(grad_ref[:, :128])
    came_s[128:] = jnp.transpose(grad_ref[:, 128:])
    spots = (came_s[9 * HOME_CAP : 10 * HOME_CAP] + 0.5).astype(jnp.int32)
    blocks, places = spots // sub, spots % sub
    hot, came = [], []
    zero = jnp.zeros((6, devices), F32)
    for j in range(HOME_CAP):
        hot.append(one_hot(iota((devices, devices), 0) == blocks[j : j + 1]))
        slot = jnp.concatenate([came_s[pl.ds(j, SENT, stride=HOME_CAP), :], zero], axis=0)
        place = places[j : j + 1]
        came.append(
            jnp.concatenate([jnp.where(place == i, slot, 0.0) for i in range(sub)], axis=0)
        )
    came = parts(jnp.concatenate(came, axis=1), 2)
    total = dot_t(jnp.concatenate(came, axis=0), jnp.concatenate(hot, axis=1))
    total = total[: sub * ROWS] + total[sub * ROWS :]
    total = jnp.concatenate([total[i * ROWS : (i + 1) * ROWS] for i in range(sub)], axis=1)
    total_s[...] = jnp.zeros_like(total_s)
    pull_back(total, old_ref[...], camera_ref, total_s)
    flags = came_s[SENT * HOME_CAP :]
    flag = jnp.max(jnp.max(flags, axis=1, keepdims=True), axis=0, keepdims=True)
    total_s[10:11] = flag + jnp.zeros((1, total_s.shape[1]), F32)
    spread_copies(total_s, out_ref)


def to_owner_body(entry_ref, lists_ref, out_ref):
    devices = out_ref.shape[0]
    rank = lists_ref[2:3]
    named = one_hot(iota((devices, rank.shape[1]), 0) == lists_ref[0:1])
    grads = entry_ref[...]
    slots = jnp.concatenate([jnp.where(rank == j, grads, 0.0) for j in range(CAP)], axis=0)
    sent = sum(dot_t(piece, named) for piece in parts(slots))
    out_ref[:, :128] = jnp.transpose(sent[:128])
    out_ref[:, 128:] = jnp.transpose(sent[128:])


def at_owner_body(grad_ref, request_ref, lists_ref, out_ref, *, gauss):
    devices = grad_ref.shape[0]
    came = jnp.concatenate(
        [jnp.transpose(grad_ref[:, :128]), jnp.transpose(grad_ref[:, 128:])], axis=0
    )
    came = jnp.concatenate([came[j * ROWS : (j + 1) * ROWS] for j in range(CAP)], axis=1)
    total = dot_t(jnp.concatenate(parts(came), axis=0), asked_hot(request_ref, gauss))
    total = total[:ROWS] + total[ROWS : 2 * ROWS] + total[2 * ROWS :]
    stack = jnp.concatenate([total, jnp.zeros_like(total)], axis=0)
    out_ref[...] = pack_blocks(stack, lists_ref[3:4, 0:gauss].astype(F32), devices, 32)


def at_home_body(came_ref, old_ref, camera_ref, out_ref, total_s):
    devices = came_ref.shape[0]
    came = jnp.transpose(came_ref[...])
    sub = old_ref.shape[1] // devices
    total = jnp.concatenate([came[i * 32 : i * 32 + ROWS] for i in range(sub)], axis=1)
    total_s[...] = jnp.zeros_like(total_s)
    pull_back(total, old_ref[...], camera_ref, total_s)
    spread_copies(total_s, out_ref)


def adam_body(
    grads_ref, old_ref, order_ref, params_ref, moment1_ref, moment2_ref, full_ref, stack_s
):
    old = old_ref[...]
    grad = (grads_ref[0] + grads_ref[1]) + (grads_ref[2] + grads_ref[3])
    grad = jnp.concatenate([grad[n : n + 12] for n in range(0, grad.shape[0], 12)], axis=1)
    full_ref[0, 0] = (jnp.max(grad[10:11]) > 0.5).astype(jnp.int32)
    grad = grad[0:10]
    moment1 = 0.9 * old[10:20] + 0.1 * grad
    moment2 = 0.99 * old[24:34] + 0.01 * grad * grad
    stack_s[...] = jnp.zeros_like(stack_s)
    stack_s[0:10] = old[0:10] - 0.01 * moment1 / (jnp.sqrt(moment2) + 1e-08)
    stack_s[16:26] = moment1
    stack_s[32:42] = moment2
    new = dot(jnp.concatenate(parts(stack_s[...]), axis=0), order_ref[...])
    new = new[:48] + new[48:96] + new[96:]
    params_ref[...] = new[0:10]
    moment1_ref[...] = new[16:26]
    moment2_ref[...] = new[32:42]


def shape(*dims, dtype=F32):
    return jax.ShapeDtypeStruct(dims, dtype)


def exchange(x):
    devices = lax.axis_size("dev")
    parcel = x.reshape(devices, -1, 128)
    return lax.all_to_all(parcel, "dev", 0, 0, tiled=True).reshape(x.shape)


def share(copies):
    return lax.all_to_all(copies, "rep", 0, 0, tiled=True)


def local(params, moment1, moment2, camera, owner, local_index, target, rehome):
    devices = lax.axis_size("dev")
    reps = lax.axis_size("rep")
    gauss = params.shape[1]
    _, tiles, depth = local_index.shape
    entries = tiles * depth
    pix = target.shape[3]
    owners = owner.reshape(1, entries)
    ids = local_index[0]
    stack = pltpu.VMEM((32, gauss), F32)
    request, lists = call(
        request_body,
        (shape(devices, 128), shape(8, entries, dtype=jnp.int32)),
        [
            pltpu.VMEM((1, entries), jnp.int32), pltpu.VMEM((tiles, depth), jnp.int32),
            pltpu.VMEM((10, gauss), F32), pltpu.VMEM((1, devices), jnp.int32), stack,
            pltpu.VMEM((devices, 128), F32), pltpu.VMEM((8, entries), jnp.int32),
            pltpu.SemaphoreType.DMA((6,)),
        ],
        hbm=(0, 1, 2, 3),
        hbm_out=(0, 1),
        vmem=60 * 1024 * 1024,
    )(owners, ids, moment2, rehome)
    request = exchange(request)
    table, blocks, lists, goal, order = call(
        table_body,
        (
            shape(ROWS, gauss), shape(256 - VALUES * CAP, devices),
            shape(8, entries, dtype=jnp.int32), shape(3, tiles, pix),
            shape(gauss, gauss, dtype=BF16),
        ),
        [stack],
        smem=(2,),
    )(params, moment1, camera, lists, target[0].transpose(1, 0, 2))
    response = call(respond_body, shape(devices, 256), [pltpu.VMEM((256, devices), F32)])(
        request, table, blocks
    )
    response = exchange(response)
    plane = pltpu.VMEM((tiles * pix, depth), F32)
    images, grads, by_entry = call(
        composite_body,
        (shape(3, tiles, pix), shape(devices, 256), shape(ROWS, entries)),
        [
            plane, plane, plane, pltpu.VMEM((2, tiles * pix, depth), BF16),
            pltpu.VMEM((ROWS, entries), F32),
        ],
    )(response, lists, goal)
    grads = exchange(grads)
    grads, old = call(
        collect_body,
        (shape(reps, gauss * 12 // 128, 128), shape(40, gauss)),
        [
            pltpu.VMEM((256, devices), F32), pltpu.VMEM((ROWS, gauss), F32),
        ],
        smem=(3,),
    )(grads, request, response, camera)
    update = call(
        adam_body,
        (shape(10, gauss),) * 3 + (shape(1, 1, dtype=jnp.int32),),
        [pltpu.VMEM((48, gauss), F32)],
        smem_out=(3,),
    )
    *out, full = update(share(grads), old, order)

    def by_owner(out, by_entry, lists, request, old, order, camera):
        sent = call(to_owner_body, shape(devices, 256))(by_entry, lists)
        sent = call(functools.partial(at_owner_body, gauss=gauss), shape(devices, 128))(
            exchange(sent), request, lists
        )
        sent = call(
            at_home_body, shape(reps, gauss * 12 // 128, 128), [pltpu.VMEM((ROWS, gauss), F32)], smem=(2,)
        )(exchange(sent), old, camera)
        return list(update(share(sent), old, order)[:3])

    _, out = lax.while_loop(
        lambda carry: carry[0] > 0,
        lambda carry: (
            jnp.int32(0), by_owner(carry[1], by_entry, lists, request, old, order, camera)
        ),
        (full[0, 0], list(out)),
    )
    return (*out, images.transpose(1, 0, 2)[None])


def solution(mesh):
    in_specs = (
        P(None, "dev"),
        P(None, "dev"),
        P(None, "dev"),
        P("rep", None),
        P("rep", "dev", None, None),
        P("rep", "dev", None),
        P("rep", "dev", None, None),
        P("dev", None),
    )
    out_specs = (P(None, "dev"), P(None, "dev"), P(None, "dev"), P("rep", "dev", None, None))
    return jax.shard_map(local, mesh=mesh, in_specs=in_specs, out_specs=out_specs, check_vma=False)
```
